512 devices in a mesh: section: 8 (over z_hi, x), expert: 64 (over y, z_lo, core).
Axes of the slice: x: 4, y: 4, z: 16 (z_hi: 2, z_lo: 8; z = z_hi * 8 + z_lo), core: 2. Of those that a mesh axis runs over, the one named last changes fastest.
Arguments:
- layer_in: bfloat16 [8, 8192, 1024], P('section', 'expert'), may hold values from -6 to 6
- upstream: bfloat16 [8, 8192, 1024], P('section', 'expert'), may hold values from -0.796875 to 0.796875
- source_lengths: int32 [64], P('expert'), may hold values from 1 to 128
- target_lengths: int32 [64], P('expert'), may hold values from 1 to 128
- expert_ids: int32 [8, 8192, 2], P('section', 'expert'), may hold values from 0 to 15, all different within a row
- gate_values: float32 [8, 8192, 2], P('section', 'expert'), may hold values from 0.2 to 1
- expert_in: bfloat16 [8, 1024, 65536], P('section', None, 'expert'), may hold values from -0.1875 to 0.1875
- expert_out: bfloat16 [8, 65536, 1024], P('section', 'expert'), may hold values from -0.09375 to 0.09375
- attention_gain: float32 [8, 1024], P('section'), may hold values from 0.5 to 1.5
- mixture_gain: float32 [8, 1024], P('section'), may hold values from 0.5 to 1.5
- final_gain: float32 [1024], replicated, may hold values from 0.5 to 1.5
Outputs:
- gate_grad: float32 [8, 8192, 2], P('section', 'expert')
- input_grad: bfloat16 [8, 8192, 1024], P('section', 'expert')
The draws below stay inside these ranges and needn't reach their ends.
Inputs may be any that keep to these rules, and one draw needn't show every extreme that they name: `expert_ids`: A token's two experts differ.
All inputs are finite; a program needn't handle non-finite values.
Results may differ from the reference program's by a relative error of at most 0.025.
The reference program's roundings to bfloat16 on the way count: a program that leaves them out, or rounds other values in their place, can miss the bound.
Values may be sent and summed in bfloat16 or wider, within the bound.
A program may use at most 64 MiB of HBM per device.

```python
import math
import jax
import jax.numpy as jnp
from jax import lax

D = 1024
HEAD_DIM = 128
HEADS = 8
FF = 4096
GROUP = 4
EXP_ST = 16
SEQ = 128
TOK_DEV = 128
CAP = 13
H_DEV = 1024
ENC = 2
FF_ALL = 65536
TOKENS = 8192
SENTS = 64
N_SECTION = 8
N_EXPERT = 64


def with_ends(array, key, low, largest):
    longest = array.shape.index(max(array.shape))
    spots = []
    for shift in (0, 1):
        where = [jax.random.randint(jax.random.fold_in(key, axis), (), 0, length) for axis, length in enumerate(array.shape)]
        where[longest] = (where[longest] + shift) % array.shape[longest]
        spots.append(tuple(where))
    return array.at[spots[0]].set(low).at[spots[1]].set(largest)


def block_scale(rng, extent, pieces, smallest, top_value):
    factor_of, own = 1.0, jax.random.fold_in(rng, 6)
    for dim, blocks in pieces:
        heights = jnp.exp(jax.random.uniform(jax.random.fold_in(own, dim), (blocks,), jnp.float32, smallest / len(pieces), top_value / len(pieces)))
        factor_of = factor_of * jnp.repeat(heights, extent[dim] // blocks).reshape([-1 if axis == dim else 1 for axis in range(len(extent))])
    return factor_of


def different_ones(own_key, rows, number_of, top, lift):
    order = jax.random.permutation(jax.random.fold_in(own_key, 1), number_of)
    boost = order
    for power in range(3):
        boost = boost * boost // number_of
    boost = boost * lift // number_of
    lots = jax.random.randint(jax.random.fold_in(own_key, 2), (rows, number_of), 0, 4096) + boost
    fixed_rows = jax.random.permutation(jax.random.fold_in(own_key, 3), rows)[jnp.arange(number_of) % rows]
    lots = jnp.where(jnp.arange(rows)[:, None] == fixed_rows[None, :], 1 << 14, lots)
    merit = lots * number_of + jnp.arange(number_of)
    return lax.top_k(merit.astype(jnp.int32), top)[1].astype(jnp.int32)


def bell_draw(stream_key, dims, scale, limit, pieces=(), kind=jnp.bfloat16):
    loudness = block_scale(stream_key, dims, pieces, -0.22, 0.18) if pieces else 1.0
    entries = jax.random.normal(stream_key, dims, jnp.float32) * scale * loudness
    return jnp.minimum(jnp.maximum(entries, -limit), limit).astype(kind)


def setup_inputs(seed: int = 0) -> dict:
    keys = jax.random.split(jax.random.key(seed), 12)
    layer_in = bell_draw(keys[0], (N_SECTION, TOKENS, D), 1.0, 6.0, ((0, 8), (1, 64)))
    upstream = bell_draw(keys[1], (N_SECTION, TOKENS, D), 0.1, 0.796875, ((0, 8), (1, 64)))
    source_lengths = with_ends(jax.random.randint(keys[2], (SENTS,), 1, SEQ + 1), jax.random.fold_in(keys[2], 1), 1, SEQ).astype(jnp.int32)
    target_lengths = with_ends(jax.random.randint(keys[3], (SENTS,), 1, SEQ + 1), jax.random.fold_in(keys[3], 1), 1, SEQ).astype(jnp.int32)
    expert_ids = different_ones(keys[4], N_SECTION * TOKENS, EXP_ST, 2, 1024).reshape((N_SECTION, TOKENS, 2))
    gate_values = jnp.clip(0.2 + 0.8 * jax.random.uniform(keys[5], (N_SECTION, TOKENS, 2), jnp.float32) ** block_scale(keys[5], (N_SECTION, TOKENS, 2), ((0, 8), (1, 64)), -0.2, 0.2), 0.2, 1.0)
    expert_in = bell_draw(keys[6], (N_SECTION, D, FF_ALL), D ** -0.5, 0.1875, ((0, 8), (2, 64)))
    expert_out = bell_draw(keys[7], (N_SECTION, FF_ALL, D), FF ** -0.5, 0.09375, ((0, 8), (1, 64)))
    attention_gain = jnp.clip(1.0 + 0.1 * jax.random.normal(keys[8], (N_SECTION, D), jnp.float32), 0.5, 1.5)
    mixture_gain = jnp.clip(1.0 + 0.1 * jax.random.normal(keys[9], (N_SECTION, D), jnp.float32), 0.5, 1.5)
    final_gain = jnp.clip(1.0 + 0.1 * jax.random.normal(keys[10], (D,), jnp.float32), 0.5, 1.5)
    return dict(layer_in=layer_in, upstream=upstream, source_lengths=source_lengths, target_lengths=target_lengths, expert_ids=expert_ids, gate_values=gate_values, expert_in=expert_in, expert_out=expert_out, attention_gain=attention_gain, mixture_gain=mixture_gain, final_gain=final_gain)


EPSILON = 1e-06
HIGH = lax.Precision.HIGHEST

def rms_scale(values, scales):
    return values * lax.rsqrt(lax.optimization_barrier(jnp.mean(values * values, axis=-1, keepdims=True)) + EPSILON) * scales

def attend(inputs, states, scales, key_mask):
    sentences = key_mask.shape[0]
    queries = rms_scale(inputs.reshape(sentences, SEQ, HEADS, HEAD_DIM), scales.reshape(HEADS, HEAD_DIM))
    memory = states.reshape(sentences, SEQ, HEADS, HEAD_DIM)
    scores = jnp.einsum('sihd,sjhd->shij', queries, memory, precision=HIGH) / math.sqrt(HEAD_DIM)
    weights = jnp.exp(scores) * key_mask[:, None, None, :]
    probability = weights / lax.optimization_barrier(jnp.sum(weights, axis=-1, keepdims=True))
    rounded = lax.optimization_barrier(probability.astype(jnp.bfloat16)).astype(jnp.float32)
    mixed = jnp.einsum('shij,sjhd->sihd', rounded, memory, precision=HIGH)
    return inputs + mixed.reshape(inputs.shape)

def expert_tables(expert_ids, gate_values):
    row_count = expert_ids.shape[0]
    experts = lax.broadcasted_iota(jnp.int32, (1, 1, EXP_ST), 2)
    chosen = (expert_ids[:, :, None] == experts).astype(jnp.int32)
    per_token = lax.optimization_barrier(jnp.sum(chosen, axis=1))
    earlier = (lax.broadcasted_iota(jnp.int32, (row_count, row_count), 1) < lax.broadcasted_iota(jnp.int32, (row_count, row_count), 0)).astype(jnp.int32)
    before = lax.optimization_barrier(jnp.sum(earlier[:, :, None] * per_token[None, :, :], axis=1))
    slot_index = lax.optimization_barrier(jnp.sum(chosen * before[:, None, :], axis=2))
    slot_iota = lax.broadcasted_iota(jnp.int32, (1, 1, 1, CAP), 3)
    matches = chosen[:, :, :, None] * (slot_index[:, :, None, None] == slot_iota).astype(jnp.int32)
    matches = matches.astype(jnp.float32).reshape(row_count, 2, EXP_ST * CAP)
    placing = lax.optimization_barrier(jnp.sum(matches, axis=1))
    weighted = lax.optimization_barrier(jnp.sum(matches * gate_values[:, :, None], axis=1))
    return (matches, placing, weighted)

def to_experts(slot_rows):
    return slot_rows.reshape(N_EXPERT, EXP_ST, CAP, D).transpose(1, 0, 2, 3).reshape(EXP_ST, N_EXPERT * CAP, D)

def to_sources(expert_rows):
    return expert_rows.reshape(EXP_ST, N_EXPERT, CAP, D).transpose(1, 0, 2, 3).reshape(N_EXPERT, EXP_ST * CAP, D)

def moe_forward(normed, tables, weights_in, weights_out):
    matches, placing, weighted = tables
    blocks = normed.reshape(N_EXPERT, TOK_DEV, D).astype(jnp.float32)
    slot_rows = jnp.einsum('bte,btd->bed', placing, blocks, precision=HIGH).astype(jnp.bfloat16)
    first = weights_in.reshape(D, EXP_ST, FF).transpose(1, 0, 2)
    second = weights_out.reshape(EXP_ST, FF, D)

    def one_expert(operands):
        expert_rows, first_layer, second_layer = operands
        hidden = jax.nn.relu(jnp.dot(expert_rows, first_layer, preferred_element_type=jnp.float32)).astype(jnp.bfloat16)
        partials = jnp.einsum('rgh,ghd->grd', hidden.reshape(-1, GROUP, H_DEV).astype(jnp.float32), second_layer.reshape(GROUP, H_DEV, D).astype(jnp.float32), precision=HIGH)
        partials = lax.optimization_barrier(partials.astype(jnp.bfloat16)).astype(jnp.float32)
        return (hidden, lax.optimization_barrier(jnp.sum(partials, axis=0)))
    hidden, summed = lax.map(one_expert, (to_experts(slot_rows), first, second))
    per_source = to_sources(summed)
    routed = jnp.einsum('bte,bed->btd', weighted, per_source, precision=HIGH).reshape(TOKENS, D)
    return (routed, per_source, hidden)

def moe_backward(upstream, tables, hidden, weights_in, weights_out):
    matches, placing, weighted = tables
    blocks = upstream.reshape(N_EXPERT, TOK_DEV, D).astype(jnp.float32)
    slot_grads = jnp.einsum('bte,btd->bed', weighted, blocks, precision=HIGH).astype(jnp.bfloat16)
    first = weights_in.reshape(D, EXP_ST, FF).transpose(1, 0, 2)
    second = weights_out.reshape(EXP_ST, FF, D)

    def one_expert(operands):
        row_grads, hidden_rows, first_layer, second_layer = operands
        hidden_grads = jnp.dot(row_grads, second_layer.T, preferred_element_type=jnp.float32)
        hidden_grads = (hidden_grads * (hidden_rows > 0)).astype(jnp.bfloat16)
        partials = jnp.einsum('rgh,dgh->grd', hidden_grads.reshape(-1, GROUP, H_DEV).astype(jnp.float32), first_layer.reshape(D, GROUP, H_DEV).astype(jnp.float32), precision=HIGH)
        partials = lax.optimization_barrier(partials.astype(jnp.bfloat16)).astype(jnp.float32)
        return lax.optimization_barrier(jnp.sum(partials, axis=0))
    summed = lax.map(one_expert, (to_experts(slot_grads), hidden, first, second))
    per_source = to_sources(summed)
    return jnp.einsum('bte,bed->btd', placing, per_source, precision=HIGH).reshape(TOKENS, D)

def gate_gradient(upstream, tables, per_source):
    matches = tables[0]
    selected = jnp.einsum('btke,bed->btkd', matches, per_source, precision=HIGH)
    blocks = upstream.reshape(N_EXPERT, TOK_DEV, 1, D).astype(jnp.float32)
    return lax.optimization_barrier(jnp.sum(blocks * selected, axis=3)).reshape(TOKENS, 2)

def reference(layer_in, upstream, source_lengths, target_lengths, expert_ids, gate_values, expert_in, expert_out, attention_gain, mixture_gain, final_gain):
    key_mask = (lax.broadcasted_iota(jnp.int32, (SENTS, SEQ), 1) < source_lengths[:, None]).astype(jnp.float32)
    loss_mask = (lax.broadcasted_iota(jnp.int32, (SENTS, SEQ), 1) < target_lengths[:, None]).astype(jnp.float32)
    loss_mask = loss_mask.reshape(TOKENS, 1)
    tables = [jax.vmap(expert_tables)(expert_ids[section_index].reshape(N_EXPERT, TOK_DEV, 2), gate_values[section_index].reshape(N_EXPERT, TOK_DEV, 2)) for section_index in range(N_SECTION)]
    records = []
    outputs = []
    for section_index in range(N_SECTION):
        inputs = layer_in[section_index].astype(jnp.float32)
        normed = rms_scale(inputs, mixture_gain[section_index]).astype(jnp.bfloat16)
        routed, per_source, hidden = moe_forward(normed, tables[section_index], expert_in[section_index], expert_out[section_index])
        records.append((inputs, per_source, hidden))
        outputs.append((inputs + routed).astype(jnp.bfloat16))
    bridge_out = outputs[ENC - 1].astype(jnp.float32)
    states = rms_scale(bridge_out, final_gain).astype(jnp.bfloat16)
    states_grad = jnp.zeros((TOKENS, D), jnp.float32)
    moe_ups = [None] * N_SECTION
    for section_index in range(ENC, N_SECTION):
        given = upstream[section_index]
        if section_index == N_SECTION - 1:
            given = (given.astype(jnp.float32) * loss_mask).astype(jnp.bfloat16)
        unused, pullback = jax.vjp(lambda values, memory: attend(values, memory, attention_gain[section_index], key_mask), outputs[section_index].astype(jnp.float32), states.astype(jnp.float32))
        cross_grad, states_part = pullback(given.astype(jnp.float32))
        states_grad = states_grad + states_part
        moe_ups[section_index] = cross_grad.astype(jnp.bfloat16)
    for section_index in range(ENC - 1):
        moe_ups[section_index] = upstream[section_index]
    unused, pullback = jax.vjp(lambda values: rms_scale(values, final_gain), bridge_out)
    moe_ups[ENC - 1] = pullback(states_grad)[0].astype(jnp.bfloat16)
    gate_grads = []
    input_grads = []
    for section_index in range(N_SECTION):
        inputs, per_source, hidden = records[section_index]
        moe_up = moe_ups[section_index]
        gate_grads.append(gate_gradient(moe_up, tables[section_index], per_source))
        normed_grad = moe_backward(moe_up, tables[section_index], hidden, expert_in[section_index], expert_out[section_index])
        unused, pullback = jax.vjp(lambda values: rms_scale(values, mixture_gain[section_index]), inputs)
        input_grads.append((moe_up.astype(jnp.float32) + pullback(normed_grad)[0]).astype(jnp.bfloat16))
    return (jnp.stack(gate_grads), jnp.stack(input_grads))
```

```python
import math

import jax
import jax.numpy as jnp
from jax import lax
from jax.experimental import pallas as pl
from jax.experimental.pallas import tpu as pltpu
from jax.sharding import PartitionSpec as P

MESH = pl.DeviceIdType.MESH
BF = jnp.bfloat16
F32 = jnp.float32
EPSILON = 1e-06
EXPERTS = 16
CAP = 13
PAD = 16
TOK = 128
D = 1024
HD = 128
ROWS = EXPERTS * PAD
BLOCK = ROWS
TILE = 256
SHIFTS = (2, 3, 1, 0)
NT = (((1,), (1,)), ((), ()))


def dot(a, b):
    return jnp.dot(a, b, preferred_element_type=F32)


def dot_nt(a, b):
    return lax.dot_general(a, b, NT, preferred_element_type=F32)


def split(v):
    high = v.astype(BF)
    return high, (v - high.astype(F32)).astype(BF)


def inverse_rms(v):
    return lax.rsqrt(jnp.mean(v * v, axis=-1, keepdims=True) + EPSILON)


def rms_back(v, g, cotangent):
    r = inverse_rms(v)
    scaled = g * cotangent
    return r * scaled - v * (r * r * r * jnp.mean(v * scaled, axis=-1, keepdims=True))


def remote(src, dst, send, recv, section, expert):
    return pltpu.make_async_remote_copy(
        src_ref=src,
        dst_ref=dst,
        send_sem=send,
        recv_sem=recv,
        device_id=(section, expert),
        device_id_type=MESH,
    )


def slot_tables(ids_ref, gates_ref):
    column = lax.broadcasted_iota(jnp.int32, (TOK, ROWS), 1)
    expert = column // PAD
    place = column - expert * PAD
    first = (ids_ref[:, 0:1] == expert).astype(F32)
    second = (ids_ref[:, 1:2] == expert).astype(F32)
    earlier = lax.broadcasted_iota(jnp.int32, (TOK, TOK), 1) < lax.broadcasted_iota(
        jnp.int32, (TOK, TOK), 0
    )
    before = dot(earlier.astype(F32).astype(BF), (first + second).astype(BF))
    kept = jnp.where(place < CAP, (before == place.astype(F32)).astype(F32), 0.0)
    first = first * kept
    second = second * kept
    weighted = first * gates_ref[:, 0:1] + second * gates_ref[:, 1:2]
    return first, second, weighted


class Exchange:
    scratch = [
        pltpu.VMEM((EXPERTS, PAD, D), BF),
        pltpu.VMEM((4, 2, 2, 4, PAD, D), BF),
        pltpu.VMEM((4, 2, 2, 4, PAD, D), BF),
        pltpu.VMEM((4, 2, 4, PAD, D), BF),
        pltpu.VMEM((4, 4, PAD, D), BF),
        pltpu.VMEM((4, 4, PAD, D), BF),
        pltpu.VMEM((4, 4, PAD, D), BF),
        pltpu.VMEM((EXPERTS, PAD, D), BF),
        pltpu.SemaphoreType.DMA((4, 4)),
        pltpu.SemaphoreType.DMA((4, 4)),
        pltpu.SemaphoreType.DMA((5, 4)),
        pltpu.SemaphoreType.DMA((5, 4)),
        pltpu.SemaphoreType.DMA((4, 4)),
        pltpu.SemaphoreType.DMA((4, 4)),
    ]

    def __init__(self, refs):
        (
            self.slots,
            self.rows,
            self.products,
            self.core_part,
            self.pair_out,
            self.pair_in,
            self.sums,
            self.back,
            self.a_send,
            self.a_recv,
            self.g_send,
            self.g_recv,
            self.f_send,
            self.f_recv,
        ) = refs
        self.section = lax.axis_index("section")
        p = lax.axis_index("expert")
        self.core = p % 2
        self.half = (p // 2) % 2
        self.ez = (p // 4) % 4
        self.ey = p // 16
        self.mine = self.ey * 4 + self.ez

    def device(self, ey, ez, half, core):
        return ((ey * 4 + ez) * 2 + half) * 2 + core

    def core_partner(self):
        return self.device(self.ey, self.ez, self.half, 1 - self.core)

    def pair_partner(self):
        return self.device(self.ey, self.ez, 1 - self.half, self.core)

    def greet(self):
        barrier = pltpu.get_barrier_semaphore()
        for dz in range(4):
            for dy in range(4):
                if dz or dy:
                    other = self.device(
                        (self.ey + dy) % 4, (self.ez + dz) % 4, self.half, self.core
                    )
                    pl.semaphore_signal(
                        barrier, inc=1, device_id=(self.section, other), device_id_type=MESH
                    )
        for other in (self.core_partner(), self.pair_partner()):
            pl.semaphore_signal(
                barrier, inc=1, device_id=(self.section, other), device_id_type=MESH
            )

    def meet(self):
        pl.semaphore_wait(pltpu.get_barrier_semaphore(), 17)

    def out_copy(self, t, dy):
        ey, ez = (self.ey + dy) % 4, (self.ez + SHIFTS[t]) % 4
        return remote(
            self.slots.at[ey * 4 + ez],
            self.rows.at[self.ez, self.core, self.half, self.ey],
            self.a_send.at[t, dy],
            self.a_recv.at[t, dy],
            self.section,
            self.device(ey, ez, self.half, self.core),
        )

    def source(self, t):
        return (self.ez + 4 - SHIFTS[t]) % 4

    def piece(self, t, kind):
        half = self.half if kind < 2 else 1 - self.half
        ref = self.rows.at[self.source(t), self.core, half]
        target = self.pair_partner() if kind == 0 else self.core_partner()
        return remote(
            ref, ref, self.g_send.at[kind, t], self.g_recv.at[kind, t], self.section, target
        )

    def core_copy(self, t):
        return remote(
            self.products.at[t, 1 - self.core],
            self.core_part.at[t],
            self.g_send.at[3, t],
            self.g_recv.at[3, t],
            self.section,
            self.core_partner(),
        )

    def pair_copy(self, t):
        return remote(
            self.pair_out.at[t],
            self.pair_in.at[t],
            self.g_send.at[4, t],
            self.g_recv.at[4, t],
            self.section,
            self.pair_partner(),
        )

    def back_copy(self, t, dy):
        ey = (self.ey + 4 - dy) % 4
        return remote(
            self.sums.at[t, ey],
            self.back.at[self.mine],
            self.f_send.at[t, dy],
            self.f_recv.at[t, dy],
            self.section,
            self.device(ey, self.source(t), self.half, self.core),
        )

    def far(self, t):
        return [dy for dy in range(4) if SHIFTS[t] or dy]

    def send_out(self):
        for t in range(4):
            for dy in self.far(t):
                self.out_copy(t, dy).start()
        self.rows[self.ez, self.core, self.half, self.ey] = self.slots[self.mine]

    def share(self, t):
        for dy in self.far(t):
            self.out_copy(t, dy).wait_recv()
        self.piece(t, 0).start()
        self.piece(t, 1).start()

    def pass_on(self, t):
        self.piece(t, 0).wait_recv()
        self.piece(t, 2).start()

    def multiply(self, t, experts):
        self.piece(t, 1).wait_recv()
        self.piece(t, 2).wait_recv()
        experts(t, self.source(t))
        self.core_copy(t).start()

    def core_sum(self, t):
        self.core_copy(t).wait_recv()
        other = 1 - self.half
        total = self.products[t, self.core, other].astype(F32) + self.core_part[t, other].astype(
            F32
        )
        self.pair_out[t] = total.astype(BF)
        self.pair_copy(t).start()

    def pair_sum(self, t):
        self.pair_copy(t).wait_recv()
        total = (
            self.products[t, self.core, self.half].astype(F32)
            + self.core_part[t, self.half].astype(F32)
            + self.pair_in[t].astype(F32)
        )
        self.sums[t] = total.astype(BF)
        for dy in self.far(t):
            self.back_copy(t, dy).start()
        if SHIFTS[t] == 0:
            self.back[self.mine] = self.sums[t, self.ey]

    def run(self, experts):
        for step in range(8):
            for stage, lag in (
                (self.share, 0),
                (self.pass_on, 1),
                (lambda t: self.multiply(t, experts), 2),
                (self.core_sum, 3),
                (self.pair_sum, 4),
            ):
                if 0 <= step - lag < 4:
                    stage(step - lag)
        for t in range(4):
            for dy in self.far(t):
                self.back_copy(t, dy).wait_recv()

    def finish(self):
        for t in range(4):
            for dy in self.far(t):
                self.out_copy(t, dy).wait_send()
                self.back_copy(t, dy).wait_send()
            for kind in range(3):
                self.piece(t, kind).wait_send()
            self.core_copy(t).wait_send()
            self.pair_copy(t).wait_send()


def forward_kernel(
    x_ref,
    ids_ref,
    gates_ref,
    mixture_ref,
    final_ref,
    w_in_hbm,
    w_out_hbm,
    moe_ref,
    states_ref,
    back_ref,
    hidden_hbm,
    w_in,
    w_out,
    hidden,
    w_sem,
    h_sem,
    *refs,
):
    ex = Exchange(refs)
    in_copy = pltpu.make_async_copy(w_in_hbm, w_in, w_sem.at[0])
    out_copy = pltpu.make_async_copy(w_out_hbm, w_out, w_sem.at[1])
    ex.greet()
    in_copy.start()
    out_copy.start()
    first, second, weighted = slot_tables(ids_ref, gates_ref)
    x = x_ref[...].astype(F32)
    normed = (x * inverse_rms(x) * mixture_ref[...]).astype(BF)
    placing_t = (first + second).T.astype(BF)
    ex.slots[...] = dot(placing_t, normed).astype(BF).reshape(EXPERTS, PAD, D)
    ex.meet()
    ex.send_out()
    in_copy.wait()
    out_copy.wait()

    def save(t, source):
        return pltpu.make_async_copy(hidden.at[source], hidden_hbm.at[source], h_sem.at[t])

    def experts(t, source):
        rows = ex.rows[source].reshape(BLOCK, D)

        def up(n, carry):
            tile = pl.ds(pl.multiple_of(n * TILE, TILE), TILE)
            hidden[source, :, tile] = jnp.maximum(dot(rows, w_in[:, tile]), 0.0).astype(BF)
            return carry

        lax.fori_loop(0, D // TILE, up, 0)
        units = hidden[source]

        def down(n, carry):
            tile = pl.ds(pl.multiple_of(n * TILE, TILE), TILE)
            part = dot(units, w_out[:, tile]).astype(BF)
            ex.products[t, :, :, :, :, tile] = part.reshape(2, 2, 4, PAD, TILE)
            return carry

        lax.fori_loop(0, D // TILE, down, 0)
        save(t, source).start()

    ex.run(experts)
    back_ref[...] = ex.back[...].reshape(ROWS, D)
    high, low = split(weighted)
    summed = back_ref[...]
    moe = (x + (dot(high, summed) + dot(low, summed))).astype(BF)
    moe_ref[...] = moe
    wide = moe.astype(F32)
    states = (wide * inverse_rms(wide) * final_ref[...]).astype(BF)
    for quarter in range(4):
        states_ref[quarter] = states[:, quarter * 256 : (quarter + 1) * 256]
    ex.finish()
    for t in range(4):
        save(t, ex.source(t)).wait()


def backward_kernel(
    x_ref,
    up_ref,
    ids_ref,
    gates_ref,
    mixture_ref,
    back_ref,
    w_in_hbm,
    w_out_hbm,
    hidden_hbm,
    gate_ref,
    grad_ref,
    w_in,
    w_out,
    hidden,
    units,
    w_sem,
    *refs,
):
    ex = Exchange(refs)
    in_copy = pltpu.make_async_copy(w_in_hbm, w_in, w_sem.at[0])
    out_copy = pltpu.make_async_copy(w_out_hbm, w_out, w_sem.at[1])
    hidden_copy = pltpu.make_async_copy(hidden_hbm, hidden, w_sem.at[2])
    ex.greet()
    in_copy.start()
    out_copy.start()
    hidden_copy.start()
    first, second, weighted = slot_tables(ids_ref, gates_ref)
    up_low = up_ref[...]
    up = up_low.astype(F32)
    high, low = split(weighted.T)
    grads = dot(high, up_low) + dot(low, up_low)
    ex.slots[...] = grads.astype(BF).reshape(EXPERTS, PAD, D)
    ex.meet()
    ex.send_out()
    summed = back_ref[...]
    gate_ref[:, 0:1] = jnp.sum(up * dot(first.astype(BF), summed), axis=1, keepdims=True)
    gate_ref[:, 1:2] = jnp.sum(up * dot(second.astype(BF), summed), axis=1, keepdims=True)
    in_copy.wait()
    out_copy.wait()
    hidden_copy.wait()

    def experts(t, source):
        rows = ex.rows[source].reshape(BLOCK, D)

        def down(n, carry):
            tile = pl.ds(pl.multiple_of(n * TILE, TILE), TILE)
            part = dot_nt(rows, w_out[tile, :])
            alive = hidden[source, :, tile].astype(F32) > 0.0
            units[:, tile] = jnp.where(alive, part, 0.0).astype(BF)
            return carry

        lax.fori_loop(0, D // TILE, down, 0)
        held = units[...]

        def across(n, carry):
            tile = pl.ds(pl.multiple_of(n * TILE, TILE), TILE)
            part = dot_nt(held, w_in[tile, :]).astype(BF)
            ex.products[t, :, :, :, :, tile] = part.reshape(2, 2, 4, PAD, TILE)
            return carry

        lax.fori_loop(0, D // TILE, across, 0)

    ex.run(experts)
    placing = (first + second).astype(BF)
    normed_grad = dot(placing, ex.back[...].reshape(ROWS, D))
    x = x_ref[...].astype(F32)
    grad_ref[...] = (up + rms_back(x, mixture_ref[...], normed_grad)).astype(BF)
    ex.finish()


def cross_kernel(
    source_len,
    target_len,
    states_ref,
    moe_ref,
    up_in_ref,
    attention_ref,
    final_ref,
    up_ref,
    held,
    terms,
    terms_in,
    cross_out,
    cross_in,
    final_out,
    final_in,
    total,
    s_send,
    s_recv,
    t_send,
    t_recv,
    x_sem,
    f_send,
    f_recv,
):
    s = lax.axis_index("section")
    p = lax.axis_index("expert")
    x = s % 4
    low_z = s < 4
    high_z = s >= 4
    bridge = s == 1
    decoder = s >= 2
    low_decoder = jnp.logical_and(low_z, decoder)
    relay = jnp.logical_and(low_z, s != 1)

    barrier = pltpu.get_barrier_semaphore()
    for d in range(1, 8):
        pl.semaphore_signal(barrier, inc=1, device_id=((s + d) % 8, p), device_id_type=MESH)
    pl.semaphore_wait(barrier, 7)

    first_sends = [(0, 0), (2, 2), (3, 3), (1, 5)]
    later_sends = [(0, 2), (1, 2), (3, 2), (0, 3), (1, 3), (2, 3)]
    sends = first_sends + later_sends

    def bridge_copy(i):
        quarter, target = sends[i]
        return remote(
            states_ref.at[quarter], held.at[quarter], s_send.at[i], s_recv.at[quarter], target, p
        )

    def onward(slot, target):
        return remote(held.at[x], held.at[x], s_send.at[slot], s_recv.at[x], target, p)

    def arrived(quarter):
        onto = held.at[quarter]
        return remote(onto, onto, s_send.at[0], s_recv.at[quarter], s, p)

    @pl.when(bridge)
    def _():
        for i in range(len(sends)):
            bridge_copy(i).start()

    @pl.when(relay)
    def _():
        arrived(x).wait_recv()
        onward(0, x + 4).start()

    @pl.when(high_z)
    def _():
        arrived(x).wait_recv()
        for d in range(1, 4):
            onward(d, 4 + (x + d) % 4).start()

    def term_high(k):
        return remote(
            terms.at[k], terms_in.at[k - 1], t_send.at[k], t_recv.at[k - 1], 4 + (x + k) % 4, p
        )

    def term_low(k):
        return remote(
            terms.at[k], terms_in.at[s - 2], t_send.at[k], t_recv.at[s - 2], (x + k) % 4, p
        )

    def term_in(slot):
        return remote(terms.at[0], terms_in.at[slot], t_send.at[0], t_recv.at[slot], s, p)

    @pl.when(decoder)
    def _():
        tokens = lax.broadcasted_iota(jnp.int32, (TOK, 1), 0)
        keys = lax.broadcasted_iota(jnp.int32, (1, TOK), 1)
        key_mask = (keys < source_len[0]).astype(F32)
        loss_mask = jnp.logical_or(tokens < target_len[0], s < 7).astype(F32)
        for k in range(4):
            j = (x + k) % 4
            if k:
                arrived(j).wait_recv()
            for h in range(2):
                lanes = pl.ds(pl.multiple_of(j * 256 + h * HD, HD), HD)
                a = moe_ref[:, lanes].astype(F32)
                m = held[j, :, h * HD : (h + 1) * HD]
                g = attention_ref[:, lanes]
                given = (up_in_ref[:, lanes].astype(F32) * loss_mask).astype(BF)
                q = a * inverse_rms(a) * g
                q_high, q_low = split(q)
                scores = (dot_nt(q_high, m) + dot_nt(q_low, m)) * (1.0 / math.sqrt(HD))
                weights = jnp.exp(scores) * key_mask
                probs = weights / jnp.sum(weights, axis=-1, keepdims=True)
                rounded = probs.astype(BF)
                d_probs = dot_nt(given, m).astype(BF).astype(F32)
                inner = jnp.sum(d_probs * probs, axis=-1, keepdims=True)
                d_scores = probs * (d_probs - inner) * (1.0 / math.sqrt(HD))
                s_high, s_low = split(d_scores)
                d_q = dot(s_high, m) + dot(s_low, m)
                t_high, t_low = split(d_scores.T)
                rounded_t = rounded.astype(F32).T.astype(BF)
                d_m = (
                    dot(rounded_t, given)
                    + dot(t_high, q_high)
                    + dot(t_high, q_low)
                    + dot(t_low, q_high)
                )
                up_ref[:, lanes] = (given.astype(F32) + rms_back(a, g, d_q)).astype(BF)
                if k == 0:
                    total[:, h * HD : (h + 1) * HD] = d_m
                else:
                    terms[k, :, h * HD : (h + 1) * HD] = d_m.astype(BF)
            if k:

                @pl.when(high_z)
                def _():
                    term_high(k).start()

                @pl.when(low_z)
                def _():
                    term_low(k).start()

    def cross_copy(target):
        return remote(cross_out, cross_in, x_sem.at[0], x_sem.at[1], target, p)

    def final_copy():
        return remote(final_out, final_in.at[x], f_send, f_recv.at[x], 1, p)

    def final_arrived(quarter):
        return remote(final_out, final_in.at[quarter], f_send, f_recv.at[quarter], s, p)

    @pl.when(high_z)
    def _():
        for slot in range(3):
            term_in(slot).wait_recv()
        summed = total[...]
        for slot in range(3):
            summed = summed + terms_in[slot].astype(F32)
        cross_out[...] = summed.astype(BF)
        cross_copy(x).start()
        cross_copy(x).wait_send()

    @pl.when(s < 2)
    def _():
        total[...] = jnp.zeros_like(total)

    @pl.when(low_z)
    def _():
        for slot in range(2):

            @pl.when(s != slot + 2)
            def _():
                term_in(slot).wait_recv()
                total[...] += terms_in[slot].astype(F32)

        cross_copy(s).wait_recv()
        total[...] += cross_in[...].astype(F32)

    @pl.when(relay)
    def _():
        final_out[...] = total[...].astype(BF)
        final_copy().start()
        final_copy().wait_send()

    @pl.when(s == 0)
    def _():
        up_ref[...] = up_in_ref[...]

    @pl.when(bridge)
    def _():
        pieces = []
        for quarter in range(4):
            if quarter == 1:
                pieces.append(total[...])
            else:
                final_arrived(quarter).wait_recv()
                pieces.append(final_in[quarter].astype(F32))
        cotangent = jnp.concatenate(pieces, axis=1)
        v = moe_ref[...].astype(F32)
        up_ref[...] = rms_back(v, final_ref[...], cotangent).astype(BF)
        for i in range(len(sends)):
            bridge_copy(i).wait_send()

    @pl.when(relay)
    def _():
        onward(0, x + 4).wait_send()

    @pl.when(high_z)
    def _():
        for d in range(1, 4):
            onward(d, 4 + (x + d) % 4).wait_send()
            term_high(d).wait_send()

    @pl.when(low_decoder)
    def _():
        for d in range(1, 4):
            term_low(d).wait_send()


VM = pl.BlockSpec(memory_space=pltpu.VMEM)
SM = pl.BlockSpec(memory_space=pltpu.SMEM)
HB = pl.BlockSpec(memory_space=pl.ANY)


def shape(dims, dtype):
    return jax.ShapeDtypeStruct(dims, dtype)


def params(number):
    return pltpu.CompilerParams(
        collective_id=number, has_side_effects=True, vmem_limit_bytes=44 * 1024 * 1024
    )


def body(
    layer_in,
    upstream,
    source_lengths,
    target_lengths,
    expert_ids,
    gate_values,
    expert_in,
    expert_out,
    attention_gain,
    mixture_gain,
    final_gain,
):
    x = layer_in[0]
    ids = expert_ids[0]
    gates = gate_values[0]
    final = final_gain.reshape(1, D)
    flops = 4 * 1024 * 1024 * 1024
    moe, states, back, hidden = pl.pallas_call(
        forward_kernel,
        out_shape=(
            shape((TOK, D), BF),
            shape((4, TOK, 256), BF),
            shape((ROWS, D), BF),
            shape((4, BLOCK, D), BF),
        ),
        in_specs=[VM] * 5 + [HB] * 2,
        out_specs=(VM, VM, VM, HB),
        scratch_shapes=[
            pltpu.VMEM((D, D), BF),
            pltpu.VMEM((D, D), BF),
            pltpu.VMEM((4, BLOCK, D), BF),
            pltpu.SemaphoreType.DMA((2,)),
            pltpu.SemaphoreType.DMA((4,)),
        ]
        + Exchange.scratch,
        compiler_params=params(0),
        cost_estimate=pl.CostEstimate(flops=flops, bytes_accessed=8 << 20, transcendentals=0),
        name="moe_forward",
    )(x, ids, gates, mixture_gain, final, expert_in[0], expert_out[0])
    moe_up = pl.pallas_call(
        cross_kernel,
        out_shape=shape((TOK, D), BF),
        in_specs=[SM, SM] + [VM] * 5,
        out_specs=VM,
        scratch_shapes=[
            pltpu.VMEM((4, TOK, 256), BF),
            pltpu.VMEM((4, TOK, 256), BF),
            pltpu.VMEM((3, TOK, 256), BF),
            pltpu.VMEM((TOK, 256), BF),
            pltpu.VMEM((TOK, 256), BF),
            pltpu.VMEM((TOK, 256), BF),
            pltpu.VMEM((4, TOK, 256), BF),
            pltpu.VMEM((TOK, 256), F32),
            pltpu.SemaphoreType.DMA((10,)),
            pltpu.SemaphoreType.DMA((4,)),
            pltpu.SemaphoreType.DMA((4,)),
            pltpu.SemaphoreType.DMA((3,)),
            pltpu.SemaphoreType.DMA((2,)),
            pltpu.SemaphoreType.DMA,
            pltpu.SemaphoreType.DMA((4,)),
        ],
        compiler_params=params(1),
        cost_estimate=pl.CostEstimate(flops=1 << 28, bytes_accessed=2 << 20, transcendentals=0),
        name="cross_attention",
    )(source_lengths, target_lengths, states, moe, upstream[0], attention_gain, final)
    gate_grad, input_grad = pl.pallas_call(
        backward_kernel,
        out_shape=(shape((TOK, 2), F32), shape((TOK, D), BF)),
        in_specs=[VM] * 6 + [HB] * 3,
        out_specs=(VM, VM),
        scratch_shapes=[
            pltpu.VMEM((D, D), BF),
            pltpu.VMEM((D, D), BF),
            pltpu.VMEM((4, BLOCK, D), BF),
            pltpu.VMEM((BLOCK, D), BF),
            pltpu.SemaphoreType.DMA((3,)),
        ]
        + Exchange.scratch,
        compiler_params=params(2),
        cost_estimate=pl.CostEstimate(flops=flops, bytes_accessed=8 << 20, transcendentals=0),
        name="moe_backward",
    )(x, moe_up, ids, gates, mixture_gain, back, expert_in[0], expert_out[0], hidden)
    return (gate_grad[None], input_grad[None])


def solution(mesh):
    in_specs = (
        P("section", "expert", None),
        P("section", "expert", None),
        P("expert"),
        P("expert"),
        P("section", "expert", None),
        P("section", "expert", None),
        P("section", None, "expert"),
        P("section", "expert", None),
        P("section", None),
        P("section", None),
        P(),
    )
    out_specs = (P("section", "expert", None), P("section", "expert", None))
    return jax.shard_map(body, mesh=mesh, in_specs=in_specs, out_specs=out_specs, check_vma=False)
```

```python
import math

import jax
import jax.numpy as jnp
from jax import lax
from jax.experimental import pallas as pl
from jax.experimental.pallas import tpu as pltpu
from jax.sharding import PartitionSpec as P

MESH = pl.DeviceIdType.MESH
BF = jnp.bfloat16
F32 = jnp.float32
EPSILON = 1e-06
EXPERTS = 16
CAP = 13
PAD = 16
TOK = 128
D = 1024
HD = 128
PACKED = 896
ROWS = EXPERTS * PAD
BLOCK = ROWS
TILE = 256
SHIFTS = (2, 3, 1, 0)
NT = (((1,), (1,)), ((), ()))


def dot(a, b):
    return jnp.dot(a, b, preferred_element_type=F32)


def dot_nt(a, b):
    return lax.dot_general(a, b, NT, preferred_element_type=F32)


def split(v):
    high = v.astype(BF)
    return high, (v - high.astype(F32)).astype(BF)


def inverse_rms(v):
    return lax.rsqrt(jnp.mean(v * v, axis=-1, keepdims=True) + EPSILON)


def rms_back(v, g, cotangent):
    r = inverse_rms(v)
    scaled = g * cotangent
    return r * scaled - v * (r * r * r * jnp.mean(v * scaled, axis=-1, keepdims=True))


def remote(src, dst, send, recv, section, expert):
    return pltpu.make_async_remote_copy(
        src_ref=src,
        dst_ref=dst,
        send_sem=send,
        recv_sem=recv,
        device_id=(section, expert),
        device_id_type=MESH,
    )


def slot_tables(ids_ref, gates_ref):
    column = lax.broadcasted_iota(jnp.int32, (TOK, ROWS), 1)
    expert = column // PAD
    place = column - expert * PAD
    first = (ids_ref[:, 0:1] == expert).astype(F32)
    second = (ids_ref[:, 1:2] == expert).astype(F32)
    earlier = lax.broadcasted_iota(jnp.int32, (TOK, TOK), 1) < lax.broadcasted_iota(
        jnp.int32, (TOK, TOK), 0
    )
    before = dot(earlier.astype(F32).astype(BF), (first + second).astype(BF))
    kept = jnp.where(place < CAP, (before == place.astype(F32)).astype(F32), 0.0)
    first = first * kept
    second = second * kept
    weighted = first * gates_ref[:, 0:1] + second * gates_ref[:, 1:2]
    return first, second, weighted


def pack_matrix():
    row = lax.broadcasted_iota(jnp.int32, (PACKED, 128), 0)
    column = lax.broadcasted_iota(jnp.int32, (PACKED, 128), 1)
    return pack_rule(row, column)


def unpack_matrix():
    row = lax.broadcasted_iota(jnp.int32, (128, PACKED), 0)
    column = lax.broadcasted_iota(jnp.int32, (128, PACKED), 1)
    return pack_rule(column, row)


def pack_rule(spare, plain):
    chunk = spare // 128
    inside = spare - chunk * 128
    block = inside // PAD
    place = inside - block * PAD
    slot = plain - block * PAD
    wanted = chunk + 7 * (place - CAP)
    hit = jnp.where(place == CAP, 1.0, jnp.where(place == CAP + 1, 1.0, 0.0))
    hit = jnp.where(wanted == slot, hit, 0.0)
    return jnp.where(wanted < CAP, hit, 0.0).astype(BF)


def pack(values, matrix):
    spare = (lax.broadcasted_iota(jnp.int32, (128, 128), 0) % PAD) >= CAP
    halves = []
    for half in range(2):
        part = values[half * 128 : (half + 1) * 128]
        moved = dot(matrix, part[:, PACKED:])
        chunks = [
            jnp.where(
                spare,
                moved[k * 128 : (k + 1) * 128],
                part[:, k * 128 : (k + 1) * 128].astype(F32),
            ).astype(BF)
            for k in range(7)
        ]
        halves.append(jnp.concatenate(chunks, axis=1))
    return jnp.concatenate(halves, axis=0)


def unpack_last(packed, matrix):
    halves = []
    for half in range(2):
        part = packed[half * 128 : (half + 1) * 128]
        stacked = jnp.concatenate([part[:, k * 128 : (k + 1) * 128] for k in range(7)], axis=0)
        halves.append(dot(matrix, stacked).astype(BF))
    return jnp.concatenate(halves, axis=0)


class Exchange:
    scratch = [
        pltpu.VMEM((EXPERTS, PAD, PACKED), BF),
        pltpu.VMEM((4, 2, 2, 4, PAD, PACKED), BF),
        pltpu.VMEM((4, 2, 2, 4, PAD, PACKED), BF),
        pltpu.VMEM((4, 2, 4, PAD, PACKED), BF),
        pltpu.VMEM((4, 2, 4, PAD, PACKED), BF),
        pltpu.VMEM((4, 2, 4, PAD, PACKED), BF),
        pltpu.VMEM((4, 2, 4, PAD, PACKED), BF),
        pltpu.VMEM((EXPERTS, PAD, PACKED), BF),
        pltpu.SemaphoreType.DMA((4, 4)),
        pltpu.SemaphoreType.DMA((4, 2, 4)),
        pltpu.SemaphoreType.DMA((4, 4)),
        pltpu.SemaphoreType.DMA((4, 4)),
        pltpu.SemaphoreType.DMA((4, 2, 4)),
        pltpu.SemaphoreType.DMA((4, 4)),
    ]

    def __init__(self, refs):
        (
            self.slots,
            self.rows,
            self.products,
            self.core_part,
            self.pair_out,
            self.pair_in,
            self.sums,
            self.back,
            self.a_send,
            self.a_recv,
            self.g_send,
            self.g_recv,
            self.f_send,
            self.f_recv,
        ) = refs
        self.section = lax.axis_index("section")
        p = lax.axis_index("expert")
        self.core = p % 2
        self.half = (p // 2) % 2
        self.ez = (p // 4) % 4
        self.ey = p // 16
        self.mine = self.ey * 4 + self.ez

    def device(self, ey, ez, half, core):
        return ((ey * 4 + ez) * 2 + half) * 2 + core

    def core_partner(self):
        return self.device(self.ey, self.ez, self.half, 1 - self.core)

    def pair_partner(self):
        return self.device(self.ey, self.ez, 1 - self.half, self.core)

    def greet(self):
        barrier = pltpu.get_barrier_semaphore()

        def signal(other):
            pl.semaphore_signal(
                barrier, inc=1, device_id=(self.section, other), device_id_type=MESH
            )

        for dz in range(4):
            for dy in range(4):
                for dh in range(2):
                    if dz or dy or dh:
                        signal(
                            self.device(
                                (self.ey + dy) % 4,
                                (self.ez + dz) % 4,
                                (self.half + dh) % 2,
                                self.core,
                            )
                        )
        signal(self.core_partner())

    def meet(self):
        pl.semaphore_wait(pltpu.get_barrier_semaphore(), 32)

    def source(self, t):
        return (self.ez + 4 - SHIFTS[t]) % 4

    def near(self, t):
        return 1 - (self.ez + 4 - SHIFTS[t]) // 4

    def far(self, t):
        return [dy for dy in range(4) if SHIFTS[t] or dy]

    def copy(self, src, dst, send, recv, target):
        return remote(src, dst, send, recv, self.section, target)

    def out_copy(self, t, dy):
        ey, ez = (self.ey + dy) % 4, (self.ez + SHIFTS[t]) % 4
        half = (self.ez + SHIFTS[t]) // 4 if SHIFTS[t] else self.half
        return self.copy(
            self.slots.at[ey * 4 + ez],
            self.rows.at[self.ez, self.core, self.half, self.ey],
            self.a_send.at[t, dy],
            self.a_recv.at[t, self.half, dy],
            self.device(ey, ez, half, self.core),
        )

    def out_arrival(self, t, half, dy):
        block = self.rows.at[self.source(t), self.core, half, (self.ey + 4 - dy) % 4]
        return self.copy(
            block, block, self.a_send.at[t, dy], self.a_recv.at[t, half, dy], self.core_partner()
        )

    def pair_share(self, t, half=None):
        block = self.rows.at[self.source(t), self.core]
        if half is not None:
            block = block.at[half]
        return self.copy(
            block, block, self.g_send.at[0, t], self.g_recv.at[0, t], self.pair_partner()
        )

    def core_share(self, t):
        block = self.rows.at[self.source(t), self.core]
        return self.copy(
            block, block, self.g_send.at[1, t], self.g_recv.at[1, t], self.core_partner()
        )

    def core_copy(self, t):
        return self.copy(
            self.products.at[t, 1 - self.core],
            self.core_part.at[t],
            self.g_send.at[2, t],
            self.g_recv.at[2, t],
            self.core_partner(),
        )

    def pair_copy(self, t, half=None):
        src, dst = self.pair_out.at[t], self.pair_in.at[t]
        if half is not None:
            src, dst = src.at[half], dst.at[half]
        return self.copy(
            src, dst, self.g_send.at[3, t], self.g_recv.at[3, t], self.pair_partner()
        )

    def back_copy(self, t, half, dy):
        ey = (self.ey + 4 - dy) % 4
        return self.copy(
            self.sums.at[t, half, ey],
            self.back.at[self.mine],
            self.f_send.at[t, half, dy],
            self.f_recv.at[t, dy],
            self.device(ey, self.source(t), half, self.core),
        )

    def back_arrival(self, t, dy):
        ey, ez = (self.ey + dy) % 4, (self.ez + SHIFTS[t]) % 4
        block = self.back.at[ey * 4 + ez]
        return self.copy(
            block, block, self.f_send.at[t, 0, dy], self.f_recv.at[t, dy], self.core_partner()
        )

    def send_out(self):
        for t in range(4):
            for dy in self.far(t):
                self.out_copy(t, dy).start()
        self.rows[self.ez, self.core, self.half, self.ey] = self.slots[self.mine]

    def share(self, t):
        if SHIFTS[t] == 0:
            for dy in self.far(t):
                self.out_arrival(t, self.half, dy).wait_recv()
            self.pair_share(t, self.half).start()
            return

        @pl.when(self.half == self.near(t))
        def _():
            for half in range(2):
                for dy in self.far(t):
                    self.out_arrival(t, half, dy).wait_recv()
            self.pair_share(t).start()
            self.core_share(t).start()

    def pass_on(self, t):
        if SHIFTS[t] == 0:
            self.pair_share(t, 1 - self.half).wait_recv()
            self.core_share(t).start()
            return

        @pl.when(self.half != self.near(t))
        def _():
            self.pair_share(t).wait_recv()
            self.core_share(t).start()

    def multiply(self, t, experts):
        self.core_share(t).wait_recv()
        experts(t, self.source(t))
        self.core_copy(t).start()

    def core_sum(self, t):
        self.core_copy(t).wait_recv()
        if SHIFTS[t] == 0:
            other = 1 - self.half
            self.pair_out[t, other] = (
                self.products[t, self.core, other].astype(F32)
                + self.core_part[t, other].astype(F32)
            ).astype(BF)
            self.pair_copy(t, other).start()
            return

        @pl.when(self.half != self.near(t))
        def _():
            self.pair_out[t] = (
                self.products[t, self.core].astype(F32) + self.core_part[t].astype(F32)
            ).astype(BF)
            self.pair_copy(t).start()

    def pair_sum(self, t):
        if SHIFTS[t] == 0:
            self.pair_copy(t, self.half).wait_recv()
            self.sums[t, self.half] = (
                self.products[t, self.core, self.half].astype(F32)
                + self.core_part[t, self.half].astype(F32)
                + self.pair_in[t, self.half].astype(F32)
            ).astype(BF)
            for dy in self.far(t):
                self.back_copy(t, self.half, dy).start()
            self.back[self.mine] = self.sums[t, self.half, self.ey]
            return

        @pl.when(self.half == self.near(t))
        def _():
            self.pair_copy(t).wait_recv()
            self.sums[t] = (
                self.products[t, self.core].astype(F32)
                + self.core_part[t].astype(F32)
                + self.pair_in[t].astype(F32)
            ).astype(BF)
            for half in range(2):
                for dy in self.far(t):
                    self.back_copy(t, half, dy).start()

    def run(self, experts):
        for step in range(8):
            for stage, lag in (
                (self.share, 0),
                (self.pass_on, 1),
                (lambda t: self.multiply(t, experts), 2),
                (self.core_sum, 3),
                (self.pair_sum, 4),
            ):
                if 0 <= step - lag < 4:
                    stage(step - lag)
        for t in range(4):
            for dy in self.far(t):
                self.back_arrival(t, dy).wait_recv()

    def finish(self):
        for t in range(4):
            for dy in self.far(t):
                self.out_copy(t, dy).wait_send()
            self.core_share(t).wait_send()
            self.core_copy(t).wait_send()
            if SHIFTS[t] == 0:
                self.pair_share(t, self.half).wait_send()
                self.pair_copy(t, 1 - self.half).wait_send()
                for dy in self.far(t):
                    self.back_copy(t, self.half, dy).wait_send()
                continue

            @pl.when(self.half == self.near(t))
            def _():
                self.pair_share(t).wait_send()
                for half in range(2):
                    for dy in self.far(t):
                        self.back_copy(t, half, dy).wait_send()

            @pl.when(self.half != self.near(t))
            def _():
                self.pair_copy(t).wait_send()

    def received(self, t, full, matrix):
        packed = self.rows[self.source(t)].reshape(BLOCK, PACKED)
        full[:, :PACKED] = packed
        full[:, PACKED:] = unpack_last(packed, matrix)

    def returned(self, matrix):
        packed = self.back[...].reshape(ROWS, PACKED)
        return jnp.concatenate([packed, unpack_last(packed, matrix)], axis=1)


def forward_kernel(
    x_ref,
    ids_ref,
    gates_ref,
    mixture_ref,
    final_ref,
    w_in_hbm,
    w_out_hbm,
    moe_ref,
    states_ref,
    back_ref,
    hidden_hbm,
    w_in,
    w_out,
    hidden,
    full,
    product,
    packing,
    unpacking,
    w_sem,
    h_sem,
    *refs,
):
    ex = Exchange(refs)
    in_copy = pltpu.make_async_copy(w_in_hbm, w_in, w_sem.at[0])
    out_copy = pltpu.make_async_copy(w_out_hbm, w_out, w_sem.at[1])
    ex.greet()
    in_copy.start()
    out_copy.start()
    first, second, weighted = slot_tables(ids_ref, gates_ref)
    x = x_ref[...].astype(F32)
    normed = (x * inverse_rms(x) * mixture_ref[...]).astype(BF)
    placing_t = (first + second).T.astype(BF)
    packing[...] = pack_matrix()
    slots = pack(dot(placing_t, normed).astype(BF), packing[...])
    ex.slots[...] = slots.reshape(EXPERTS, PAD, PACKED)
    ex.meet()
    ex.send_out()
    unpacking[...] = unpack_matrix()
    in_copy.wait()
    out_copy.wait()

    def save(t, source):
        return pltpu.make_async_copy(hidden.at[source], hidden_hbm.at[source], h_sem.at[t])

    def experts(t, source):
        ex.received(t, full, unpacking[...])
        rows = full[...]

        def up(n, carry):
            tile = pl.ds(pl.multiple_of(n * TILE, TILE), TILE)
            hidden[source, :, tile] = jnp.maximum(dot(rows, w_in[:, tile]), 0.0).astype(BF)
            return carry

        lax.fori_loop(0, D // TILE, up, 0)
        units = hidden[source]

        def down(n, carry):
            tile = pl.ds(pl.multiple_of(n * TILE, TILE), TILE)
            product[:, tile] = dot(units, w_out[:, tile]).astype(BF)
            return carry

        lax.fori_loop(0, D // TILE, down, 0)
        ex.products[t] = pack(product[...], packing[...]).reshape(2, 2, 4, PAD, PACKED)
        save(t, source).start()

    ex.run(experts)
    summed = ex.returned(unpacking[...])
    back_ref[...] = summed
    high, low = split(weighted)
    moe = (x + (dot(high, summed) + dot(low, summed))).astype(BF)
    moe_ref[...] = moe
    wide = moe.astype(F32)
    states = (wide * inverse_rms(wide) * final_ref[...]).astype(BF)
    for quarter in range(4):
        states_ref[quarter] = states[:, quarter * 256 : (quarter + 1) * 256]
    ex.finish()
    for t in range(4):
        save(t, ex.source(t)).wait()


def backward_kernel(
    x_ref,
    up_ref,
    ids_ref,
    gates_ref,
    mixture_ref,
    back_ref,
    w_in_hbm,
    w_out_hbm,
    hidden_hbm,
    gate_ref,
    grad_ref,
    w_in,
    w_out,
    hidden,
    units,
    full,
    product,
    packing,
    unpacking,
    w_sem,
    *refs,
):
    ex = Exchange(refs)
    in_copy = pltpu.make_async_copy(w_in_hbm, w_in, w_sem.at[0])
    out_copy = pltpu.make_async_copy(w_out_hbm, w_out, w_sem.at[1])
    hidden_copy = pltpu.make_async_copy(hidden_hbm, hidden, w_sem.at[2])
    ex.greet()
    in_copy.start()
    out_copy.start()
    hidden_copy.start()
    first, second, weighted = slot_tables(ids_ref, gates_ref)
    up_low = up_ref[...]
    up = up_low.astype(F32)
    high, low = split(weighted.T)
    grads = dot(high, up_low) + dot(low, up_low)
    packing[...] = pack_matrix()
    ex.slots[...] = pack(grads.astype(BF), packing[...]).reshape(EXPERTS, PAD, PACKED)
    ex.meet()
    ex.send_out()
    unpacking[...] = unpack_matrix()
    summed = back_ref[...]
    gate_ref[:, 0:1] = jnp.sum(up * dot(first.astype(BF), summed), axis=1, keepdims=True)
    gate_ref[:, 1:2] = jnp.sum(up * dot(second.astype(BF), summed), axis=1, keepdims=True)
    in_copy.wait()
    out_copy.wait()
    hidden_copy.wait()

    def experts(t, source):
        ex.received(t, full, unpacking[...])
        rows = full[...]

        def down(n, carry):
            tile = pl.ds(pl.multiple_of(n * TILE, TILE), TILE)
            part = dot_nt(rows, w_out[tile, :])
            alive = hidden[source, :, tile].astype(F32) > 0.0
            units[:, tile] = jnp.where(alive, part, 0.0).astype(BF)
            return carry

        lax.fori_loop(0, D // TILE, down, 0)
        held = units[...]

        def across(n, carry):
            tile = pl.ds(pl.multiple_of(n * TILE, TILE), TILE)
            product[:, tile] = dot_nt(held, w_in[tile, :]).astype(BF)
            return carry

        lax.fori_loop(0, D // TILE, across, 0)
        ex.products[t] = pack(product[...], packing[...]).reshape(2, 2, 4, PAD, PACKED)

    ex.run(experts)
    placing = (first + second).astype(BF)
    normed_grad = dot(placing, ex.returned(unpacking[...]))
    x = x_ref[...].astype(F32)
    grad_ref[...] = (up + rms_back(x, mixture_ref[...], normed_grad)).astype(BF)
    ex.finish()


def cross_kernel(
    source_len,
    target_len,
    states_ref,
    moe_ref,
    up_in_ref,
    attention_ref,
    final_ref,
    up_ref,
    held,
    terms,
    terms_in,
    cross_out,
    cross_in,
    final_out,
    final_in,
    total,
    s_send,
    s_recv,
    t_send,
    t_recv,
    x_sem,
    f_send,
    f_recv,
):
    s = lax.axis_index("section")
    p = lax.axis_index("expert")
    x = s % 4
    low_z = s < 4
    high_z = s >= 4
    bridge = s == 1
    decoder = s >= 2
    low_decoder = jnp.logical_and(low_z, decoder)
    relay = jnp.logical_and(low_z, s != 1)

    barrier = pltpu.get_barrier_semaphore()
    for d in range(1, 8):
        pl.semaphore_signal(barrier, inc=1, device_id=((s + d) % 8, p), device_id_type=MESH)
    pl.semaphore_wait(barrier, 7)

    first_sends = [(0, 0), (2, 2), (3, 3), (1, 5)]
    later_sends = [(0, 2), (1, 2), (3, 2), (0, 3), (1, 3), (2, 3)]
    sends = first_sends + later_sends

    def bridge_copy(i):
        quarter, target = sends[i]
        return remote(
            states_ref.at[quarter], held.at[quarter], s_send.at[i], s_recv.at[quarter], target, p
        )

    def onward(slot, target):
        return remote(held.at[x], held.at[x], s_send.at[slot], s_recv.at[x], target, p)

    def arrived(quarter):
        onto = held.at[quarter]
        return remote(onto, onto, s_send.at[0], s_recv.at[quarter], s, p)

    @pl.when(bridge)
    def _():
        for i in range(len(sends)):
            bridge_copy(i).start()

    @pl.when(relay)
    def _():
        arrived(x).wait_recv()
        onward(0, x + 4).start()

    @pl.when(high_z)
    def _():
        arrived(x).wait_recv()
        for d in range(1, 4):
            onward(d, 4 + (x + d) % 4).start()

    def term_high(k):
        return remote(
            terms.at[k], terms_in.at[k - 1], t_send.at[k], t_recv.at[k - 1], 4 + (x + k) % 4, p
        )

    def term_low(k):
        return remote(
            terms.at[k], terms_in.at[s - 2], t_send.at[k], t_recv.at[s - 2], (x + k) % 4, p
        )

    def term_in(slot):
        return remote(terms.at[0], terms_in.at[slot], t_send.at[0], t_recv.at[slot], s, p)

    @pl.when(decoder)
    def _():
        tokens = lax.broadcasted_iota(jnp.int32, (TOK, 1), 0)
        keys = lax.broadcasted_iota(jnp.int32, (1, TOK), 1)
        key_mask = (keys < source_len[0]).astype(F32)
        loss_mask = jnp.logical_or(tokens < target_len[0], s < 7).astype(F32)
        for k in range(4):
            j = (x + k) % 4
            if k:
                arrived(j).wait_recv()
            for h in range(2):
                lanes = pl.ds(pl.multiple_of(j * 256 + h * HD, HD), HD)
                a = moe_ref[:, lanes].astype(F32)
                m = held[j, :, h * HD : (h + 1) * HD]
                g = attention_ref[:, lanes]
                given = (up_in_ref[:, lanes].astype(F32) * loss_mask).astype(BF)
                q = a * inverse_rms(a) * g
                q_high, q_low = split(q)
                scores = (dot_nt(q_high, m) + dot_nt(q_low, m)) * (1.0 / math.sqrt(HD))
                weights = jnp.exp(scores) * key_mask
                probs = weights / jnp.sum(weights, axis=-1, keepdims=True)
                rounded = probs.astype(BF)
                d_probs = dot_nt(given, m).astype(BF).astype(F32)
                inner = jnp.sum(d_probs * probs, axis=-1, keepdims=True)
                d_scores = probs * (d_probs - inner) * (1.0 / math.sqrt(HD))
                s_high, s_low = split(d_scores)
                d_q = dot(s_high, m) + dot(s_low, m)
                t_high, t_low = split(d_scores.T)
                rounded_t = rounded.astype(F32).T.astype(BF)
                d_m = (
                    dot(rounded_t, given)
                    + dot(t_high, q_high)
                    + dot(t_high, q_low)
                    + dot(t_low, q_high)
                )
                up_ref[:, lanes] = (given.astype(F32) + rms_back(a, g, d_q)).astype(BF)
                if k == 0:
                    total[:, h * HD : (h + 1) * HD] = d_m
                else:
                    terms[k, :, h * HD : (h + 1) * HD] = d_m.astype(BF)
            if k:

                @pl.when(high_z)
                def _():
                    term_high(k).start()

                @pl.when(low_z)
                def _():
                    term_low(k).start()

    def cross_copy(target):
        return remote(cross_out, cross_in, x_sem.at[0], x_sem.at[1], target, p)

    def final_copy():
        return remote(final_out, final_in.at[x], f_send, f_recv.at[x], 1, p)

    def final_arrived(quarter):
        return remote(final_out, final_in.at[quarter], f_send, f_recv.at[quarter], s, p)

    @pl.when(high_z)
    def _():
        for slot in range(3):
            term_in(slot).wait_recv()
        summed = total[...]
        for slot in range(3):
            summed = summed + terms_in[slot].astype(F32)
        cross_out[...] = summed.astype(BF)
        cross_copy(x).start()
        cross_copy(x).wait_send()

    @pl.when(s < 2)
    def _():
        total[...] = jnp.zeros_like(total)

    @pl.when(low_z)
    def _():
        for slot in range(2):

            @pl.when(s != slot + 2)
            def _():
                term_in(slot).wait_recv()
                total[...] += terms_in[slot].astype(F32)

        cross_copy(s).wait_recv()
        total[...] += cross_in[...].astype(F32)

    @pl.when(relay)
    def _():
        final_out[...] = total[...].astype(BF)
        final_copy().start()
        final_copy().wait_send()

    @pl.when(s == 0)
    def _():
        up_ref[...] = up_in_ref[...]

    @pl.when(bridge)
    def _():
        pieces = []
        for quarter in range(4):
            if quarter == 1:
                pieces.append(total[...])
            else:
                final_arrived(quarter).wait_recv()
                pieces.append(final_in[quarter].astype(F32))
        cotangent = jnp.concatenate(pieces, axis=1)
        v = moe_ref[...].astype(F32)
        up_ref[...] = rms_back(v, final_ref[...], cotangent).astype(BF)
        for i in range(len(sends)):
            bridge_copy(i).wait_send()

    @pl.when(relay)
    def _():
        onward(0, x + 4).wait_send()

    @pl.when(high_z)
    def _():
        for d in range(1, 4):
            onward(d, 4 + (x + d) % 4).wait_send()
            term_high(d).wait_send()

    @pl.when(low_decoder)
    def _():
        for d in range(1, 4):
            term_low(d).wait_send()


VM = pl.BlockSpec(memory_space=pltpu.VMEM)
SM = pl.BlockSpec(memory_space=pltpu.SMEM)
HB = pl.BlockSpec(memory_space=pl.ANY)


def shape(dims, dtype):
    return jax.ShapeDtypeStruct(dims, dtype)


def params(number):
    return pltpu.CompilerParams(
        collective_id=number, has_side_effects=True, vmem_limit_bytes=60 * 1024 * 1024
    )


def body(
    layer_in,
    upstream,
    source_lengths,
    target_lengths,
    expert_ids,
    gate_values,
    expert_in,
    expert_out,
    attention_gain,
    mixture_gain,
    final_gain,
):
    x = layer_in[0]
    ids = expert_ids[0]
    gates = gate_values[0]
    final = final_gain.reshape(1, D)
    flops = 4 * 1024 * 1024 * 1024
    moe, states, back, hidden = pl.pallas_call(
        forward_kernel,
        out_shape=(
            shape((TOK, D), BF),
            shape((4, TOK, 256), BF),
            shape((ROWS, D), BF),
            shape((4, BLOCK, D), BF),
        ),
        in_specs=[VM] * 5 + [HB] * 2,
        out_specs=(VM, VM, VM, HB),
        scratch_shapes=[
            pltpu.VMEM((D, D), BF),
            pltpu.VMEM((D, D), BF),
            pltpu.VMEM((4, BLOCK, D), BF),
            pltpu.VMEM((BLOCK, D), BF),
            pltpu.VMEM((BLOCK, D), BF),
            pltpu.VMEM((PACKED, 128), BF),
            pltpu.VMEM((128, PACKED), BF),
            pltpu.SemaphoreType.DMA((2,)),
            pltpu.SemaphoreType.DMA((4,)),
        ]
        + Exchange.scratch,
        compiler_params=params(0),
        cost_estimate=pl.CostEstimate(flops=flops, bytes_accessed=8 << 20, transcendentals=0),
        name="moe_forward",
    )(x, ids, gates, mixture_gain, final, expert_in[0], expert_out[0])
    moe_up = pl.pallas_call(
        cross_kernel,
        out_shape=shape((TOK, D), BF),
        in_specs=[SM, SM] + [VM] * 5,
        out_specs=VM,
        scratch_shapes=[
            pltpu.VMEM((4, TOK, 256), BF),
            pltpu.VMEM((4, TOK, 256), BF),
            pltpu.VMEM((3, TOK, 256), BF),
            pltpu.VMEM((TOK, 256), BF),
            pltpu.VMEM((TOK, 256), BF),
            pltpu.VMEM((TOK, 256), BF),
            pltpu.VMEM((4, TOK, 256), BF),
            pltpu.VMEM((TOK, 256), F32),
            pltpu.SemaphoreType.DMA((10,)),
            pltpu.SemaphoreType.DMA((4,)),
            pltpu.SemaphoreType.DMA((4,)),
            pltpu.SemaphoreType.DMA((3,)),
            pltpu.SemaphoreType.DMA((2,)),
            pltpu.SemaphoreType.DMA,
            pltpu.SemaphoreType.DMA((4,)),
        ],
        compiler_params=params(1),
        cost_estimate=pl.CostEstimate(flops=1 << 28, bytes_accessed=2 << 20, transcendentals=0),
        name="cross_attention",
    )(source_lengths, target_lengths, states, moe, upstream[0], attention_gain, final)
    gate_grad, input_grad = pl.pallas_call(
        backward_kernel,
        out_shape=(shape((TOK, 2), F32), shape((TOK, D), BF)),
        in_specs=[VM] * 6 + [HB] * 3,
        out_specs=(VM, VM),
        scratch_shapes=[
            pltpu.VMEM((D, D), BF),
            pltpu.VMEM((D, D), BF),
            pltpu.VMEM((4, BLOCK, D), BF),
            pltpu.VMEM((BLOCK, D), BF),
            pltpu.VMEM((BLOCK, D), BF),
            pltpu.VMEM((BLOCK, D), BF),
            pltpu.VMEM((PACKED, 128), BF),
            pltpu.VMEM((128, PACKED), BF),
            pltpu.SemaphoreType.DMA((3,)),
        ]
        + Exchange.scratch,
        compiler_params=params(2),
        cost_estimate=pl.CostEstimate(flops=flops, bytes_accessed=8 << 20, transcendentals=0),
        name="moe_backward",
    )(x, moe_up, ids, gates, mixture_gain, back, expert_in[0], expert_out[0], hidden)
    return (gate_grad[None], input_grad[None])


def solution(mesh):
    in_specs = (
        P("section", "expert", None),
        P("section", "expert", None),
        P("expert"),
        P("expert"),
        P("section", "expert", None),
        P("section", "expert", None),
        P("section", None, "expert"),
        P("section", "expert", None),
        P("section", None),
        P("section", None),
        P(),
    )
    out_specs = (P("section", "expert", None), P("section", "expert", None))
    return jax.shard_map(body, mesh=mesh, in_specs=in_specs, out_specs=out_specs, check_vma=False)
```

```python
import math

import jax
import jax.numpy as jnp
from jax import lax
from jax.experimental import pallas as pl
from jax.experimental.pallas import tpu as pltpu
from jax.sharding import PartitionSpec as P

MESH = pl.DeviceIdType.MESH
BF = jnp.bfloat16
F32 = jnp.float32
EPSILON = 1e-06
EXPERTS = 16
CAP = 13
PAD = 16
TOK = 128
D = 1024
HD = 128
PACKED = 896
ROWS = EXPERTS * PAD
BLOCK = ROWS
TILE = 256
SHIFTS = (2, 3, 1, 0)
NT = (((1,), (1,)), ((), ()))


def dot(a, b):
    return jnp.dot(a, b, preferred_element_type=F32)


def dot_nt(a, b):
    return lax.dot_general(a, b, NT, preferred_element_type=F32)


def split(v):
    high = v.astype(BF)
    return high, (v - high.astype(F32)).astype(BF)


def inverse_rms(v):
    return lax.rsqrt(jnp.mean(v * v, axis=-1, keepdims=True) + EPSILON)


def rms_back(v, g, cotangent):
    r = inverse_rms(v)
    scaled = g * cotangent
    return r * scaled - v * (r * r * r * jnp.mean(v * scaled, axis=-1, keepdims=True))


def remote(src, dst, send, recv, section, expert):
    return pltpu.make_async_remote_copy(
        src_ref=src,
        dst_ref=dst,
        send_sem=send,
        recv_sem=recv,
        device_id=(section, expert),
        device_id_type=MESH,
    )


def spread(row):
    column = jnp.broadcast_to(row, (TOK, TOK)).T
    return jnp.concatenate([column, column], axis=1)


def slot_tables(ids_ref, gates_ref):
    column = lax.broadcasted_iota(jnp.int32, (TOK, ROWS), 1)
    expert = column // PAD
    place = column - expert * PAD
    first = (spread(ids_ref[0:1, :].astype(F32)) == expert.astype(F32)).astype(F32)
    second = (spread(ids_ref[1:2, :].astype(F32)) == expert.astype(F32)).astype(F32)
    earlier = lax.broadcasted_iota(jnp.int32, (TOK, TOK), 1) < lax.broadcasted_iota(
        jnp.int32, (TOK, TOK), 0
    )
    before = dot(earlier.astype(F32).astype(BF), (first + second).astype(BF))
    kept = jnp.where(place < CAP, (before == place.astype(F32)).astype(F32), 0.0)
    first = first * kept
    second = second * kept
    weighted = first * spread(gates_ref[0:1, :]) + second * spread(gates_ref[1:2, :])
    return first, second, weighted


def pack_matrix():
    row = lax.broadcasted_iota(jnp.int32, (PACKED, 128), 0)
    column = lax.broadcasted_iota(jnp.int32, (PACKED, 128), 1)
    return pack_rule(row, column)


def unpack_matrix():
    row = lax.broadcasted_iota(jnp.int32, (128, PACKED), 0)
    column = lax.broadcasted_iota(jnp.int32, (128, PACKED), 1)
    return pack_rule(column, row)


def pack_rule(spare, plain):
    chunk = spare // 128
    inside = spare - chunk * 128
    block = inside // PAD
    place = inside - block * PAD
    slot = plain - block * PAD
    wanted = chunk + 7 * (place - CAP)
    hit = jnp.where(place == CAP, 1.0, jnp.where(place == CAP + 1, 1.0, 0.0))
    hit = jnp.where(wanted == slot, hit, 0.0)
    return jnp.where(wanted < CAP, hit, 0.0).astype(BF)


def pack(values, matrix):
    spare = (lax.broadcasted_iota(jnp.int32, (128, 128), 0) % PAD) >= CAP
    halves = []
    for half in range(2):
        part = values[half * 128 : (half + 1) * 128]
        moved = dot(matrix, part[:, PACKED:])
        chunks = [
            jnp.where(
                spare,
                moved[k * 128 : (k + 1) * 128],
                part[:, k * 128 : (k + 1) * 128].astype(F32),
            ).astype(BF)
            for k in range(7)
        ]
        halves.append(jnp.concatenate(chunks, axis=1))
    return jnp.concatenate(halves, axis=0)


def unpack_last(packed, matrix):
    halves = []
    for half in range(2):
        part = packed[half * 128 : (half + 1) * 128]
        stacked = jnp.concatenate([part[:, k * 128 : (k + 1) * 128] for k in range(7)], axis=0)
        halves.append(dot(matrix, stacked).astype(BF))
    return jnp.concatenate(halves, axis=0)


class Exchange:
    scratch = [
        pltpu.VMEM((EXPERTS, PAD, PACKED), BF),
        pltpu.VMEM((4, 2, 2, 4, PAD, PACKED), BF),
        pltpu.VMEM((4, 2, 2, 4, PAD, PACKED), BF),
        pltpu.VMEM((4, 2, 4, PAD, PACKED), BF),
        pltpu.VMEM((4, 2, 4, PAD, PACKED), BF),
        pltpu.VMEM((4, 2, 4, PAD, PACKED), BF),
        pltpu.VMEM((4, 2, 4, PAD, PACKED), BF),
        pltpu.VMEM((EXPERTS, PAD, PACKED), BF),
        pltpu.SemaphoreType.DMA((4, 4)),
        pltpu.SemaphoreType.DMA((4, 2, 4)),
        pltpu.SemaphoreType.DMA((4, 4)),
        pltpu.SemaphoreType.DMA((4, 4)),
        pltpu.SemaphoreType.DMA((4, 2, 4)),
        pltpu.SemaphoreType.DMA((4, 4)),
    ]

    def __init__(self, refs):
        (
            self.slots,
            self.rows,
            self.products,
            self.core_part,
            self.pair_out,
            self.pair_in,
            self.sums,
            self.back,
            self.a_send,
            self.a_recv,
            self.g_send,
            self.g_recv,
            self.f_send,
            self.f_recv,
        ) = refs
        self.section = lax.axis_index("section")
        p = lax.axis_index("expert")
        self.core = p % 2
        self.half = (p // 2) % 2
        self.ez = (p // 4) % 4
        self.ey = p // 16
        self.mine = self.ey * 4 + self.ez

    def device(self, ey, ez, half, core):
        return ((ey * 4 + ez) * 2 + half) * 2 + core

    def core_partner(self):
        return self.device(self.ey, self.ez, self.half, 1 - self.core)

    def pair_partner(self):
        return self.device(self.ey, self.ez, 1 - self.half, self.core)

    def greet(self):
        barrier = pltpu.get_barrier_semaphore()

        def signal(other):
            pl.semaphore_signal(
                barrier, inc=1, device_id=(self.section, other), device_id_type=MESH
            )

        for dz in range(4):
            for dy in range(4):
                for dh in range(2):
                    if dz or dy or dh:
                        signal(
                            self.device(
                                (self.ey + dy) % 4,
                                (self.ez + dz) % 4,
                                (self.half + dh) % 2,
                                self.core,
                            )
                        )
        signal(self.core_partner())

    def source(self, t):
        return (self.ez + 4 - SHIFTS[t]) % 4

    def near(self, t):
        return 1 - (self.ez + 4 - SHIFTS[t]) // 4

    def far(self, t):
        return [dy for dy in range(4) if SHIFTS[t] or dy]

    def copy(self, src, dst, send, recv, target):
        return remote(src, dst, send, recv, self.section, target)

    def out_copy(self, t, dy):
        ey, ez = (self.ey + dy) % 4, (self.ez + SHIFTS[t]) % 4
        half = (self.ez + SHIFTS[t]) // 4 if SHIFTS[t] else self.half
        return self.copy(
            self.slots.at[ey * 4 + ez],
            self.rows.at[self.ez, self.core, self.half, self.ey],
            self.a_send.at[t, dy],
            self.a_recv.at[t, self.half, dy],
            self.device(ey, ez, half, self.core),
        )

    def out_arrival(self, t, half, dy):
        block = self.rows.at[self.source(t), self.core, half, (self.ey + 4 - dy) % 4]
        return self.copy(
            block, block, self.a_send.at[t, dy], self.a_recv.at[t, half, dy], self.core_partner()
        )

    def pair_share(self, t, half=None):
        block = self.rows.at[self.source(t), self.core]
        if half is not None:
            block = block.at[half]
        return self.copy(
            block, block, self.g_send.at[0, t], self.g_recv.at[0, t], self.pair_partner()
        )

    def core_share(self, t):
        block = self.rows.at[self.source(t), self.core]
        return self.copy(
            block, block, self.g_send.at[1, t], self.g_recv.at[1, t], self.core_partner()
        )

    def core_copy(self, t):
        return self.copy(
            self.products.at[t, 1 - self.core],
            self.core_part.at[t],
            self.g_send.at[2, t],
            self.g_recv.at[2, t],
            self.core_partner(),
        )

    def pair_copy(self, t, half=None):
        src, dst = self.pair_out.at[t], self.pair_in.at[t]
        if half is not None:
            src, dst = src.at[half], dst.at[half]
        return self.copy(
            src, dst, self.g_send.at[3, t], self.g_recv.at[3, t], self.pair_partner()
        )

    def back_copy(self, t, half, dy):
        ey = (self.ey + 4 - dy) % 4
        return self.copy(
            self.sums.at[t, half, ey],
            self.back.at[self.mine],
            self.f_send.at[t, half, dy],
            self.f_recv.at[t, dy],
            self.device(ey, self.source(t), half, self.core),
        )

    def back_arrival(self, t, dy):
        ey, ez = (self.ey + dy) % 4, (self.ez + SHIFTS[t]) % 4
        block = self.back.at[ey * 4 + ez]
        return self.copy(
            block, block, self.f_send.at[t, 0, dy], self.f_recv.at[t, dy], self.core_partner()
        )

    def send_out(self):
        for t in range(4):
            for dy in self.far(t):
                self.out_copy(t, dy).start()
        self.rows[self.ez, self.core, self.half, self.ey] = self.slots[self.mine]

    def share(self, t):
        if SHIFTS[t] == 0:
            for dy in self.far(t):
                self.out_arrival(t, self.half, dy).wait_recv()
            self.pair_share(t, self.half).start()
            return

        @pl.when(self.half == self.near(t))
        def _():
            for half in range(2):
                for dy in self.far(t):
                    self.out_arrival(t, half, dy).wait_recv()
            self.pair_share(t).start()
            self.core_share(t).start()

    def pass_on(self, t):
        if SHIFTS[t] == 0:
            self.pair_share(t, 1 - self.half).wait_recv()
            self.core_share(t).start()
            return

        @pl.when(self.half != self.near(t))
        def _():
            self.pair_share(t).wait_recv()
            self.core_share(t).start()

    def multiply(self, t, experts):
        self.core_share(t).wait_recv()
        experts(t, self.source(t))
        self.core_copy(t).start()

    def core_sum(self, t):
        self.core_copy(t).wait_recv()
        if SHIFTS[t] == 0:
            other = 1 - self.half
            self.pair_out[t, other] = (
                self.products[t, self.core, other].astype(F32)
                + self.core_part[t, other].astype(F32)
            ).astype(BF)
            self.pair_copy(t, other).start()
            return

        @pl.when(self.half != self.near(t))
        def _():
            self.pair_out[t] = (
                self.products[t, self.core].astype(F32) + self.core_part[t].astype(F32)
            ).astype(BF)
            self.pair_copy(t).start()

    def pair_sum(self, t):
        if SHIFTS[t] == 0:
            self.pair_copy(t, self.half).wait_recv()
            self.sums[t, self.half] = (
                self.products[t, self.core, self.half].astype(F32)
                + self.core_part[t, self.half].astype(F32)
                + self.pair_in[t, self.half].astype(F32)
            ).astype(BF)
            for dy in self.far(t):
                self.back_copy(t, self.half, dy).start()
            self.back[self.mine] = self.sums[t, self.half, self.ey]
            return

        @pl.when(self.half == self.near(t))
        def _():
            self.pair_copy(t).wait_recv()
            self.sums[t] = (
                self.products[t, self.core].astype(F32)
                + self.core_part[t].astype(F32)
                + self.pair_in[t].astype(F32)
            ).astype(BF)
            for half in range(2):
                for dy in self.far(t):
                    self.back_copy(t, half, dy).start()

    def run(self, experts):
        for step in range(8):
            for stage, lag in (
                (self.share, 0),
                (self.pass_on, 1),
                (lambda t: self.multiply(t, experts), 2),
                (self.core_sum, 3),
                (self.pair_sum, 4),
            ):
                if 0 <= step - lag < 4:
                    stage(step - lag)
        for t in range(4):
            for dy in self.far(t):
                self.back_arrival(t, dy).wait_recv()

    def finish(self):
        for t in range(4):
            for dy in self.far(t):
                self.out_copy(t, dy).wait_send()
            self.core_share(t).wait_send()
            self.core_copy(t).wait_send()
            if SHIFTS[t] == 0:
                self.pair_share(t, self.half).wait_send()
                self.pair_copy(t, 1 - self.half).wait_send()
                for dy in self.far(t):
                    self.back_copy(t, self.half, dy).wait_send()
                continue

            @pl.when(self.half == self.near(t))
            def _():
                self.pair_share(t).wait_send()
                for half in range(2):
                    for dy in self.far(t):
                        self.back_copy(t, half, dy).wait_send()

            @pl.when(self.half != self.near(t))
            def _():
                self.pair_copy(t).wait_send()

    def received(self, t, full, matrix):
        packed = self.rows[self.source(t)].reshape(BLOCK, PACKED)
        full[:, :PACKED] = packed
        full[:, PACKED:] = unpack_last(packed, matrix)

    def returned(self, matrix):
        packed = self.back[...].reshape(ROWS, PACKED)
        return jnp.concatenate([packed, unpack_last(packed, matrix)], axis=1)


CROSS_SCRATCH = [
    pltpu.VMEM((4, TOK, 256), BF),
    pltpu.VMEM((4, TOK, 256), BF),
    pltpu.VMEM((3, TOK, 256), BF),
    pltpu.VMEM((TOK, 256), BF),
    pltpu.VMEM((TOK, 256), BF),
    pltpu.VMEM((TOK, 256), BF),
    pltpu.VMEM((4, TOK, 256), BF),
    pltpu.VMEM((TOK, 256), F32),
    pltpu.SemaphoreType.DMA((10,)),
    pltpu.SemaphoreType.DMA((4,)),
    pltpu.SemaphoreType.DMA((4,)),
    pltpu.SemaphoreType.DMA((3,)),
    pltpu.SemaphoreType.DMA((2,)),
    pltpu.SemaphoreType.DMA,
    pltpu.SemaphoreType.DMA((4,)),
]


def cross_part(
    source_len,
    target_len,
    states_ref,
    moe_ref,
    up_in_ref,
    attention_ref,
    final_ref,
    up_ref,
    held,
    terms,
    terms_in,
    cross_out,
    cross_in,
    final_out,
    final_in,
    total,
    s_send,
    s_recv,
    t_send,
    t_recv,
    x_sem,
    f_send,
    f_recv,
):
    s = lax.axis_index("section")
    p = lax.axis_index("expert")
    x = s % 4
    low_z = s < 4
    high_z = s >= 4
    bridge = s == 1
    decoder = s >= 2
    low_decoder = jnp.logical_and(low_z, decoder)
    relay = jnp.logical_and(low_z, s != 1)

    first_sends = [(0, 0), (2, 2), (3, 3), (1, 5)]
    later_sends = [(0, 2), (1, 2), (3, 2), (0, 3), (1, 3), (2, 3)]
    sends = first_sends + later_sends

    def bridge_copy(i):
        quarter, target = sends[i]
        return remote(
            states_ref.at[quarter], held.at[quarter], s_send.at[i], s_recv.at[quarter], target, p
        )

    def onward(slot, target):
        return remote(held.at[x], held.at[x], s_send.at[slot], s_recv.at[x], target, p)

    def arrived(quarter):
        onto = held.at[quarter]
        return remote(onto, onto, s_send.at[0], s_recv.at[quarter], s, p)

    @pl.when(bridge)
    def _():
        for i in range(len(sends)):
            bridge_copy(i).start()

    @pl.when(relay)
    def _():
        arrived(x).wait_recv()
        onward(0, x + 4).start()

    @pl.when(high_z)
    def _():
        arrived(x).wait_recv()
        for d in range(1, 4):
            onward(d, 4 + (x + d) % 4).start()

    def term_high(k):
        return remote(
            terms.at[k], terms_in.at[k - 1], t_send.at[k], t_recv.at[k - 1], 4 + (x + k) % 4, p
        )

    def term_low(k):
        return remote(
            terms.at[k], terms_in.at[s - 2], t_send.at[k], t_recv.at[s - 2], (x + k) % 4, p
        )

    def term_in(slot):
        return remote(terms.at[0], terms_in.at[slot], t_send.at[0], t_recv.at[slot], s, p)

    @pl.when(decoder)
    def _():
        tokens = lax.broadcasted_iota(jnp.int32, (TOK, 1), 0)
        keys = lax.broadcasted_iota(jnp.int32, (1, TOK), 1)
        key_mask = (keys < source_len[0]).astype(F32)
        loss_mask = jnp.logical_or(tokens < target_len[0], s < 7).astype(F32)
        for k in range(4):
            j = (x + k) % 4
            if k:
                arrived(j).wait_recv()
            for h in range(2):
                lanes = pl.ds(pl.multiple_of(j * 256 + h * HD, HD), HD)
                a = moe_ref[:, lanes].astype(F32)
                m = held[j, :, h * HD : (h + 1) * HD]
                g = attention_ref[:, lanes]
                given = (up_in_ref[:, lanes].astype(F32) * loss_mask).astype(BF)
                q = a * inverse_rms(a) * g
                q_high, q_low = split(q)
                scores = (dot_nt(q_high, m) + dot_nt(q_low, m)) * (1.0 / math.sqrt(HD))
                weights = jnp.exp(scores) * key_mask
                probs = weights / jnp.sum(weights, axis=-1, keepdims=True)
                rounded = probs.astype(BF)
                d_probs = dot_nt(given, m).astype(BF).astype(F32)
                inner = jnp.sum(d_probs * probs, axis=-1, keepdims=True)
                d_scores = probs * (d_probs - inner) * (1.0 / math.sqrt(HD))
                s_high, s_low = split(d_scores)
                d_q = dot(s_high, m) + dot(s_low, m)
                t_high, t_low = split(d_scores.T)
                rounded_t = rounded.astype(F32).T.astype(BF)
                d_m = (
                    dot(rounded_t, given)
                    + dot(t_high, q_high)
                    + dot(t_high, q_low)
                    + dot(t_low, q_high)
                )
                up_ref[:, lanes] = (given.astype(F32) + rms_back(a, g, d_q)).astype(BF)
                if k == 0:
                    total[:, h * HD : (h + 1) * HD] = d_m
                else:
                    terms[k, :, h * HD : (h + 1) * HD] = d_m.astype(BF)
            if k:

                @pl.when(high_z)
                def _():
                    term_high(k).start()

                @pl.when(low_z)
                def _():
                    term_low(k).start()

    def cross_copy(target):
        return remote(cross_out, cross_in, x_sem.at[0], x_sem.at[1], target, p)

    def final_copy():
        return remote(final_out, final_in.at[x], f_send, f_recv.at[x], 1, p)

    def final_arrived(quarter):
        return remote(final_out, final_in.at[quarter], f_send, f_recv.at[quarter], s, p)

    @pl.when(high_z)
    def _():
        for slot in range(3):
            term_in(slot).wait_recv()
        summed = total[...]
        for slot in range(3):
            summed = summed + terms_in[slot].astype(F32)
        cross_out[...] = summed.astype(BF)
        cross_copy(x).start()
        cross_copy(x).wait_send()

    @pl.when(s < 2)
    def _():
        total[...] = jnp.zeros_like(total)

    @pl.when(low_z)
    def _():
        for slot in range(2):

            @pl.when(s != slot + 2)
            def _():
                term_in(slot).wait_recv()
                total[...] += terms_in[slot].astype(F32)

        cross_copy(s).wait_recv()
        total[...] += cross_in[...].astype(F32)

    @pl.when(relay)
    def _():
        final_out[...] = total[...].astype(BF)
        final_copy().start()
        final_copy().wait_send()

    @pl.when(s == 0)
    def _():
        up_ref[...] = up_in_ref[...]

    @pl.when(bridge)
    def _():
        pieces = []
        for quarter in range(4):
            if quarter == 1:
                pieces.append(total[...])
            else:
                final_arrived(quarter).wait_recv()
                pieces.append(final_in[quarter].astype(F32))
        cotangent = jnp.concatenate(pieces, axis=1)
        v = moe_ref[...].astype(F32)
        up_ref[...] = rms_back(v, final_ref[...], cotangent).astype(BF)
        for i in range(len(sends)):
            bridge_copy(i).wait_send()

    @pl.when(relay)
    def _():
        onward(0, x + 4).wait_send()

    @pl.when(high_z)
    def _():
        for d in range(1, 4):
            onward(d, 4 + (x + d) % 4).wait_send()
            term_high(d).wait_send()

    @pl.when(low_decoder)
    def _():
        for d in range(1, 4):
            term_low(d).wait_send()


def whole_kernel(
    source_len,
    target_len,
    x_ref,
    up_in_ref,
    ids_ref,
    gates_ref,
    attention_ref,
    mixture_ref,
    final_ref,
    w_in_hbm,
    w_out_hbm,
    gate_ref,
    grad_ref,
    w_in,
    w_out,
    hidden,
    units,
    full,
    product,
    packing,
    unpacking,
    matches,
    weights,
    moe_ref,
    states_ref,
    summed_ref,
    up_ref,
    w_sem,
    *refs,
):
    cross_refs = refs[: len(CROSS_SCRATCH)]
    refs = refs[len(CROSS_SCRATCH) :]
    ahead = Exchange(refs[: len(refs) // 2])
    behind = Exchange(refs[len(refs) // 2 :])
    in_copy = pltpu.make_async_copy(w_in_hbm, w_in, w_sem.at[0])
    out_copy = pltpu.make_async_copy(w_out_hbm, w_out, w_sem.at[1])
    barrier = pltpu.get_barrier_semaphore()
    s = lax.axis_index("section")
    p = lax.axis_index("expert")
    ahead.greet()
    for d in range(1, 8):
        pl.semaphore_signal(barrier, inc=1, device_id=((s + d) % 8, p), device_id_type=MESH)
    in_copy.start()
    out_copy.start()

    first, second, weighted = slot_tables(ids_ref, gates_ref)
    x = x_ref[...].astype(F32)
    normed = (x * inverse_rms(x) * mixture_ref[...]).astype(BF)
    placing_t = (first + second).T.astype(BF)
    packing[...] = pack_matrix()
    slots = pack(dot(placing_t, normed).astype(BF), packing[...])
    ahead.slots[...] = slots.reshape(EXPERTS, PAD, PACKED)
    pl.semaphore_wait(barrier, 39)
    ahead.send_out()
    matches[0] = first.astype(BF)
    matches[1] = second.astype(BF)
    weights[...] = weighted
    unpacking[...] = unpack_matrix()
    in_copy.wait()
    out_copy.wait()

    def experts(t, source):
        ahead.received(t, full, unpacking[...])
        rows = full[...]

        def up(n, carry):
            tile = pl.ds(pl.multiple_of(n * TILE, TILE), TILE)
            hidden[source, :, tile] = jnp.maximum(dot(rows, w_in[:, tile]), 0.0).astype(BF)
            return carry

        lax.fori_loop(0, D // TILE, up, 0)
        held = hidden[source]

        def down(n, carry):
            tile = pl.ds(pl.multiple_of(n * TILE, TILE), TILE)
            product[:, tile] = dot(held, w_out[:, tile]).astype(BF)
            return carry

        lax.fori_loop(0, D // TILE, down, 0)
        ahead.products[t] = pack(product[...], packing[...]).reshape(2, 2, 4, PAD, PACKED)

    ahead.run(experts)
    summed = ahead.returned(unpacking[...])
    summed_ref[...] = summed
    high, low = split(weights[...])
    moe = (x_ref[...].astype(F32) + (dot(high, summed) + dot(low, summed))).astype(BF)
    moe_ref[...] = moe

    @pl.when(s == 1)
    def _():
        wide = moe_ref[...].astype(F32)
        states = (wide * inverse_rms(wide) * final_ref[...]).astype(BF)
        for quarter in range(4):
            states_ref[quarter] = states[:, quarter * 256 : (quarter + 1) * 256]

    cross_part(
        source_len,
        target_len,
        states_ref,
        moe_ref,
        up_in_ref,
        attention_ref,
        final_ref,
        up_ref,
        *cross_refs,
    )

    up_low = up_ref[...]
    high, low = split(weights[...].T)
    grads = dot(high, up_low) + dot(low, up_low)
    behind.slots[...] = pack(grads.astype(BF), packing[...]).reshape(EXPERTS, PAD, PACKED)
    behind.send_out()
    wide_up = up_low.astype(F32)
    for choice in range(2):
        chosen = dot(matches[choice], summed_ref[...])
        column = jnp.sum(wide_up * chosen, axis=1, keepdims=True)
        gate_ref[choice : choice + 1, :] = jnp.broadcast_to(column, (TOK, TOK)).T[0:1, :]

    def experts_back(t, source):
        behind.received(t, full, unpacking[...])
        rows = full[...]

        def down(n, carry):
            tile = pl.ds(pl.multiple_of(n * TILE, TILE), TILE)
            part = dot_nt(rows, w_out[tile, :])
            alive = hidden[source, :, tile].astype(F32) > 0.0
            units[:, tile] = jnp.where(alive, part, 0.0).astype(BF)
            return carry

        lax.fori_loop(0, D // TILE, down, 0)
        held = units[...]

        def across(n, carry):
            tile = pl.ds(pl.multiple_of(n * TILE, TILE), TILE)
            product[:, tile] = dot_nt(held, w_in[tile, :]).astype(BF)
            return carry

        lax.fori_loop(0, D // TILE, across, 0)
        behind.products[t] = pack(product[...], packing[...]).reshape(2, 2, 4, PAD, PACKED)

    behind.run(experts_back)
    placing = (matches[0].astype(F32) + matches[1].astype(F32)).astype(BF)
    normed_grad = dot(placing, behind.returned(unpacking[...]))
    back = rms_back(x_ref[...].astype(F32), mixture_ref[...], normed_grad)
    grad_ref[...] = (up_ref[...].astype(F32) + back).astype(BF)
    ahead.finish()
    behind.finish()


VM = pl.BlockSpec(memory_space=pltpu.VMEM)
SM = pl.BlockSpec(memory_space=pltpu.SMEM)
HB = pl.BlockSpec(memory_space=pl.ANY)


def shape(dims, dtype):
    return jax.ShapeDtypeStruct(dims, dtype)


def params(number):
    return pltpu.CompilerParams(
        collective_id=number, has_side_effects=True, vmem_limit_bytes=60 * 1024 * 1024
    )


def body(
    layer_in,
    upstream,
    source_lengths,
    target_lengths,
    expert_ids,
    gate_values,
    expert_in,
    expert_out,
    attention_gain,
    mixture_gain,
    final_gain,
):
    vmem = pltpu.VMEM
    gate_grad, input_grad = pl.pallas_call(
        whole_kernel,
        out_shape=(shape((2, TOK), F32), shape((TOK, D), BF)),
        in_specs=[SM] * 2 + [VM] * 7 + [HB] * 2,
        out_specs=(VM, VM),
        scratch_shapes=[
            vmem((D, D), BF),
            vmem((D, D), BF),
            vmem((4, BLOCK, D), BF),
            vmem((BLOCK, D), BF),
            vmem((BLOCK, D), BF),
            vmem((BLOCK, D), BF),
            vmem((PACKED, 128), BF),
            vmem((128, PACKED), BF),
            vmem((2, TOK, ROWS), BF),
            vmem((TOK, ROWS), F32),
            vmem((TOK, D), BF),
            vmem((4, TOK, 256), BF),
            vmem((ROWS, D), BF),
            vmem((TOK, D), BF),
            pltpu.SemaphoreType.DMA((2,)),
        ]
        + CROSS_SCRATCH
        + Exchange.scratch
        + Exchange.scratch,
        compiler_params=params(0),
        cost_estimate=pl.CostEstimate(
            flops=8 * 1024 * 1024 * 1024, bytes_accessed=8 << 20, transcendentals=0
        ),
        name="mixture_step",
    )(
        source_lengths,
        target_lengths,
        layer_in[0],
        upstream[0],
        expert_ids[0].T,
        gate_values[0].T,
        attention_gain,
        mixture_gain,
        final_gain.reshape(1, D),
        expert_in[0],
        expert_out[0],
    )
    return (gate_grad.T[None], input_grad[None])


def solution(mesh):
    in_specs = (
        P("section", "expert", None),
        P("section", "expert", None),
        P("expert"),
        P("expert"),
        P("section", "expert", None),
        P("section", "expert", None),
        P("section", None, "expert"),
        P("section", "expert", None),
        P("section", None),
        P("section", None),
        P(),
    )
    out_specs = (P("section", "expert", None), P("section", "expert", None))
    return jax.shard_map(body, mesh=mesh, in_specs=in_specs, out_specs=out_specs, check_vma=False)
```

```python
import math

import jax
import jax.numpy as jnp
from jax import lax
from jax.experimental import pallas as pl
from jax.experimental.pallas import tpu as pltpu
from jax.sharding import PartitionSpec as P

MESH = pl.DeviceIdType.MESH
BF = jnp.bfloat16
F32 = jnp.float32
EPSILON = 1e-06
EXPERTS = 16
CAP = 13
PAD = 16
TOK = 128
D = 1024
HD = 128
PACKED = 896
ROWS = EXPERTS * PAD
BLOCK = ROWS
TILE = 256
SHIFTS = (2, 3, 1, 0)
NT = (((1,), (1,)), ((), ()))


def dot(a, b):
    return jnp.dot(a, b, preferred_element_type=F32)


def dot_nt(a, b):
    return lax.dot_general(a, b, NT, preferred_element_type=F32)


def split(v):
    high = v.astype(BF)
    return high, (v - high.astype(F32)).astype(BF)


def inverse_rms(v):
    return lax.rsqrt(jnp.mean(v * v, axis=-1, keepdims=True) + EPSILON)


def rms_back(v, g, cotangent):
    r = inverse_rms(v)
    scaled = g * cotangent
    return r * scaled - v * (r * r * r * jnp.mean(v * scaled, axis=-1, keepdims=True))


def remote(src, dst, send, recv, section, expert):
    return pltpu.make_async_remote_copy(
        src_ref=src,
        dst_ref=dst,
        send_sem=send,
        recv_sem=recv,
        device_id=(section, expert),
        device_id_type=MESH,
    )


def spread(row):
    column = jnp.broadcast_to(row, (TOK, TOK)).T
    return jnp.concatenate([column, column], axis=1)


def slot_tables(ids_ref, gates_ref):
    column = lax.broadcasted_iota(jnp.int32, (TOK, ROWS), 1)
    expert = column // PAD
    place = column - expert * PAD
    first = (spread(ids_ref[0:1, :].astype(F32)) == expert.astype(F32)).astype(F32)
    second = (spread(ids_ref[1:2, :].astype(F32)) == expert.astype(F32)).astype(F32)
    earlier = lax.broadcasted_iota(jnp.int32, (TOK, TOK), 1) < lax.broadcasted_iota(
        jnp.int32, (TOK, TOK), 0
    )
    before = dot(earlier.astype(F32).astype(BF), (first + second).astype(BF))
    kept = jnp.where(place < CAP, (before == place.astype(F32)).astype(F32), 0.0)
    first = first * kept
    second = second * kept
    weighted = first * spread(gates_ref[0:1, :]) + second * spread(gates_ref[1:2, :])
    return first, second, weighted


def pack_matrix():
    row = lax.broadcasted_iota(jnp.int32, (PACKED, 128), 0)
    column = lax.broadcasted_iota(jnp.int32, (PACKED, 128), 1)
    return pack_rule(row, column)


def unpack_matrix():
    row = lax.broadcasted_iota(jnp.int32, (128, PACKED), 0)
    column = lax.broadcasted_iota(jnp.int32, (128, PACKED), 1)
    return pack_rule(column, row)


def pack_rule(spare, plain):
    chunk = spare // 128
    inside = spare - chunk * 128
    block = inside // PAD
    place = inside - block * PAD
    slot = plain - block * PAD
    wanted = chunk + 7 * (place - CAP)
    hit = jnp.where(place == CAP, 1.0, jnp.where(place == CAP + 1, 1.0, 0.0))
    hit = jnp.where(wanted == slot, hit, 0.0)
    return jnp.where(wanted < CAP, hit, 0.0).astype(BF)


def pack(values, matrix):
    spare = (lax.broadcasted_iota(jnp.int32, (128, 128), 0) % PAD) >= CAP
    halves = []
    for half in range(2):
        part = values[half * 128 : (half + 1) * 128]
        moved = dot(matrix, part[:, PACKED:])
        chunks = [
            jnp.where(
                spare,
                moved[k * 128 : (k + 1) * 128],
                part[:, k * 128 : (k + 1) * 128].astype(F32),
            ).astype(BF)
            for k in range(7)
        ]
        halves.append(jnp.concatenate(chunks, axis=1))
    return jnp.concatenate(halves, axis=0)


def unpack_last(packed, matrix):
    halves = []
    for half in range(2):
        part = packed[half * 128 : (half + 1) * 128]
        stacked = jnp.concatenate([part[:, k * 128 : (k + 1) * 128] for k in range(7)], axis=0)
        halves.append(dot(matrix, stacked).astype(BF))
    return jnp.concatenate(halves, axis=0)


class Exchange:
    scratch = [
        pltpu.VMEM((EXPERTS, PAD, PACKED), BF),
        pltpu.VMEM((4, 2, 2, 4, PAD, PACKED), BF),
        pltpu.VMEM((4, 2, 2, 4, PAD, PACKED), BF),
        pltpu.VMEM((4, 2, 4, PAD, PACKED), BF),
        pltpu.VMEM((4, 2, 4, PAD, PACKED), BF),
        pltpu.VMEM((4, 2, 4, PAD, PACKED), BF),
        pltpu.VMEM((4, 2, 4, PAD, PACKED), BF),
        pltpu.VMEM((EXPERTS, PAD, PACKED), BF),
        pltpu.SemaphoreType.DMA((4, 4)),
        pltpu.SemaphoreType.DMA((4, 2, 4)),
        pltpu.SemaphoreType.DMA((4, 4)),
        pltpu.SemaphoreType.DMA((4, 4)),
        pltpu.SemaphoreType.DMA((4, 2, 4)),
        pltpu.SemaphoreType.DMA((4, 4)),
    ]

    def __init__(self, refs):
        (
            self.slots,
            self.rows,
            self.products,
            self.core_part,
            self.pair_out,
            self.pair_in,
            self.sums,
            self.back,
            self.a_send,
            self.a_recv,
            self.g_send,
            self.g_recv,
            self.f_send,
            self.f_recv,
        ) = refs
        self.section = lax.axis_index("section")
        p = lax.axis_index("expert")
        self.core = p % 2
        self.half = (p // 2) % 2
        self.ez = (p // 4) % 4
        self.ey = p // 16
        self.mine = self.ey * 4 + self.ez

    def device(self, ey, ez, half, core):
        return ((ey * 4 + ez) * 2 + half) * 2 + core

    def core_partner(self):
        return self.device(self.ey, self.ez, self.half, 1 - self.core)

    def pair_partner(self):
        return self.device(self.ey, self.ez, 1 - self.half, self.core)

    def greet(self):
        barrier = pltpu.get_barrier_semaphore()

        def signal(other):
            pl.semaphore_signal(
                barrier, inc=1, device_id=(self.section, other), device_id_type=MESH
            )

        for dz in range(4):
            for dy in range(4):
                for dh in range(2):
                    if dz or dy or dh:
                        signal(
                            self.device(
                                (self.ey + dy) % 4,
                                (self.ez + dz) % 4,
                                (self.half + dh) % 2,
                                self.core,
                            )
                        )
        signal(self.core_partner())

    def source(self, t):
        return (self.ez + 4 - SHIFTS[t]) % 4

    def near(self, t):
        return 1 - (self.ez + 4 - SHIFTS[t]) // 4

    def far(self, t):
        return [dy for dy in range(4) if SHIFTS[t] or dy]

    def copy(self, src, dst, send, recv, target):
        return remote(src, dst, send, recv, self.section, target)

    def out_copy(self, t, dy):
        ey, ez = (self.ey + dy) % 4, (self.ez + SHIFTS[t]) % 4
        half = (self.ez + SHIFTS[t]) // 4 if SHIFTS[t] else self.half
        return self.copy(
            self.slots.at[ey * 4 + ez],
            self.rows.at[self.ez, self.core, self.half, self.ey],
            self.a_send.at[t, dy],
            self.a_recv.at[t, self.half, dy],
            self.device(ey, ez, half, self.core),
        )

    def out_arrival(self, t, half, dy):
        block = self.rows.at[self.source(t), self.core, half, (self.ey + 4 - dy) % 4]
        return self.copy(
            block, block, self.a_send.at[t, dy], self.a_recv.at[t, half, dy], self.core_partner()
        )

    def pair_share(self, t, half=None):
        block = self.rows.at[self.source(t), self.core]
        if half is not None:
            block = block.at[half]
        return self.copy(
            block, block, self.g_send.at[0, t], self.g_recv.at[0, t], self.pair_partner()
        )

    def core_share(self, t):
        block = self.rows.at[self.source(t), self.core]
        return self.copy(
            block, block, self.g_send.at[1, t], self.g_recv.at[1, t], self.core_partner()
        )

    def core_copy(self, t):
        return self.copy(
            self.products.at[t, 1 - self.core],
            self.core_part.at[t],
            self.g_send.at[2, t],
            self.g_recv.at[2, t],
            self.core_partner(),
        )

    def pair_copy(self, t, half=None):
        src, dst = self.pair_out.at[t], self.pair_in.at[t]
        if half is not None:
            src, dst = src.at[half], dst.at[half]
        return self.copy(
            src, dst, self.g_send.at[3, t], self.g_recv.at[3, t], self.pair_partner()
        )

    def back_copy(self, t, half, dy):
        ey = (self.ey + 4 - dy) % 4
        return self.copy(
            self.sums.at[t, half, ey],
            self.back.at[self.mine],
            self.f_send.at[t, half, dy],
            self.f_recv.at[t, dy],
            self.device(ey, self.source(t), half, self.core),
        )

    def back_arrival(self, t, dy):
        ey, ez = (self.ey + dy) % 4, (self.ez + SHIFTS[t]) % 4
        block = self.back.at[ey * 4 + ez]
        return self.copy(
            block, block, self.f_send.at[t, 0, dy], self.f_recv.at[t, dy], self.core_partner()
        )

    def send_out(self):
        for t in range(4):
            for dy in self.far(t):
                self.out_copy(t, dy).start()
        self.rows[self.ez, self.core, self.half, self.ey] = self.slots[self.mine]

    def share(self, t):
        if SHIFTS[t] == 0:
            for dy in self.far(t):
                self.out_arrival(t, self.half, dy).wait_recv()
            self.pair_share(t, self.half).start()
            return

        @pl.when(self.half == self.near(t))
        def _():
            for half in range(2):
                for dy in self.far(t):
                    self.out_arrival(t, half, dy).wait_recv()
            self.pair_share(t).start()
            self.core_share(t).start()

    def pass_on(self, t):
        if SHIFTS[t] == 0:
            self.pair_share(t, 1 - self.half).wait_recv()
            self.core_share(t).start()
            return

        @pl.when(self.half != self.near(t))
        def _():
            self.pair_share(t).wait_recv()
            self.core_share(t).start()

    def multiply(self, t, experts):
        self.core_share(t).wait_recv()
        experts(t, self.source(t))
        self.core_copy(t).start()

    def core_sum(self, t):
        self.core_copy(t).wait_recv()
        if SHIFTS[t] == 0:
            other = 1 - self.half
            self.pair_out[t, other] = (
                self.products[t, self.core, other].astype(F32)
                + self.core_part[t, other].astype(F32)
            ).astype(BF)
            self.pair_copy(t, other).start()
            return

        @pl.when(self.half != self.near(t))
        def _():
            self.pair_out[t] = (
                self.products[t, self.core].astype(F32) + self.core_part[t].astype(F32)
            ).astype(BF)
            self.pair_copy(t).start()

    def pair_sum(self, t):
        if SHIFTS[t] == 0:
            self.pair_copy(t, self.half).wait_recv()
            self.sums[t, self.half] = (
                self.products[t, self.core, self.half].astype(F32)
                + self.core_part[t, self.half].astype(F32)
                + self.pair_in[t, self.half].astype(F32)
            ).astype(BF)
            for dy in self.far(t):
                self.back_copy(t, self.half, dy).start()
            self.back[self.mine] = self.sums[t, self.half, self.ey]
            return

        @pl.when(self.half == self.near(t))
        def _():
            self.pair_copy(t).wait_recv()
            self.sums[t] = (
                self.products[t, self.core].astype(F32)
                + self.core_part[t].astype(F32)
                + self.pair_in[t].astype(F32)
            ).astype(BF)
            for half in range(2):
                for dy in self.far(t):
                    self.back_copy(t, half, dy).start()

    def run(self, experts):
        for step in range(8):
            for stage, lag in (
                (self.share, 0),
                (self.pass_on, 1),
                (lambda t: self.multiply(t, experts), 2),
                (self.core_sum, 3),
                (self.pair_sum, 4),
            ):
                if 0 <= step - lag < 4:
                    stage(step - lag)
        for t in range(4):
            for dy in self.far(t):
                self.back_arrival(t, dy).wait_recv()

    def finish(self):
        for t in range(4):
            for dy in self.far(t):
                self.out_copy(t, dy).wait_send()
            self.core_share(t).wait_send()
            self.core_copy(t).wait_send()
            if SHIFTS[t] == 0:
                self.pair_share(t, self.half).wait_send()
                self.pair_copy(t, 1 - self.half).wait_send()
                for dy in self.far(t):
                    self.back_copy(t, self.half, dy).wait_send()
                continue

            @pl.when(self.half == self.near(t))
            def _():
                self.pair_share(t).wait_send()
                for half in range(2):
                    for dy in self.far(t):
                        self.back_copy(t, half, dy).wait_send()

            @pl.when(self.half != self.near(t))
            def _():
                self.pair_copy(t).wait_send()

    def received(self, t, full, matrix):
        packed = self.rows[self.source(t)].reshape(BLOCK, PACKED)
        full[:, :PACKED] = packed
        full[:, PACKED:] = unpack_last(packed, matrix)

    def returned(self, matrix):
        packed = self.back[...].reshape(ROWS, PACKED)
        return jnp.concatenate([packed, unpack_last(packed, matrix)], axis=1)


CROSS_SCRATCH = [
    pltpu.VMEM((4, TOK, 256), BF),
    pltpu.VMEM((4, TOK, 256), BF),
    pltpu.VMEM((3, TOK, 256), BF),
    pltpu.VMEM((TOK, 256), BF),
    pltpu.VMEM((TOK, 256), BF),
    pltpu.VMEM((TOK, 256), BF),
    pltpu.VMEM((4, TOK, 256), BF),
    pltpu.VMEM((TOK, 256), F32),
    pltpu.VMEM((TOK, 256), BF),
    pltpu.VMEM((4, TOK, 256), BF),
    pltpu.SemaphoreType.DMA((12,)),
    pltpu.SemaphoreType.DMA((4,)),
    pltpu.SemaphoreType.DMA((4,)),
    pltpu.SemaphoreType.DMA((3,)),
    pltpu.SemaphoreType.DMA((2,)),
    pltpu.SemaphoreType.DMA,
    pltpu.SemaphoreType.DMA((4,)),
    pltpu.SemaphoreType.DMA((2,)),
    pltpu.SemaphoreType.DMA,
    pltpu.SemaphoreType.DMA((4,)),
]


def cross_part(
    source_len,
    target_len,
    states_ref,
    moe_ref,
    up_in_ref,
    attention_ref,
    final_ref,
    up_ref,
    held,
    terms,
    terms_in,
    cross_out,
    cross_in,
    final_out,
    final_in,
    total,
    relayed,
    far_in,
    s_send,
    s_recv,
    t_send,
    t_recv,
    x_sem,
    f_send,
    f_recv,
    y_sem,
    r_send,
    r_recv,
):
    s = lax.axis_index("section")
    p = lax.axis_index("expert")
    side = p + 2 - 4 * ((p // 2) % 2)
    x = s % 4
    low_z = s < 4
    high_z = s >= 4
    bridge = s == 1
    decoder = s >= 2
    low_decoder = jnp.logical_and(low_z, decoder)
    sender = jnp.logical_and(low_z, s != 1)

    relays = (0, 2, 3, 1)
    direct = ((2, 2), (3, 3), (3, 2), (0, 3), (0, 2), (1, 3), (1, 2), (2, 3))

    def relay_copy(i):
        return remote(
            states_ref.at[relays[i]], relayed, s_send.at[i], y_sem.at[1], relays[i], side
        )

    def direct_copy(i):
        quarter, target = direct[i]
        return remote(
            states_ref.at[quarter],
            held.at[quarter],
            s_send.at[4 + i],
            s_recv.at[quarter],
            target,
            p,
        )

    def relay_on():
        return remote(relayed, held.at[x], y_sem.at[0], s_recv.at[x], x + 4, side)

    def onward(slot, target):
        return remote(held.at[x], held.at[x], s_send.at[slot], s_recv.at[x], target, p)

    def arrived(quarter):
        onto = held.at[quarter]
        return remote(onto, onto, s_send.at[0], s_recv.at[quarter], s, side)

    @pl.when(bridge)
    def _():
        for i in range(len(relays)):
            relay_copy(i).start()
        for i in range(len(direct)):
            direct_copy(i).start()

    @pl.when(low_z)
    def _():
        remote(relayed, relayed, y_sem.at[0], y_sem.at[1], s, side).wait_recv()
        relay_on().start()

    @pl.when(low_decoder)
    def _():
        arrived(x).wait_recv()

    @pl.when(high_z)
    def _():
        arrived(x).wait_recv()
        for d in range(1, 4):
            onward(d, 4 + (x + d) % 4).start()

    def term_high(k):
        return remote(
            terms.at[k], terms_in.at[k - 1], t_send.at[k], t_recv.at[k - 1], 4 + (x + k) % 4, p
        )

    def term_low(k):
        return remote(
            terms.at[k], terms_in.at[s - 2], t_send.at[k], t_recv.at[s - 2], (x + k) % 4, p
        )

    def term_in(slot):
        return remote(terms.at[0], terms_in.at[slot], t_send.at[0], t_recv.at[slot], s, side)

    @pl.when(decoder)
    def _():
        tokens = lax.broadcasted_iota(jnp.int32, (TOK, 1), 0)
        keys = lax.broadcasted_iota(jnp.int32, (1, TOK), 1)
        key_mask = (keys < source_len[0]).astype(F32)
        loss_mask = jnp.logical_or(tokens < target_len[0], s < 7).astype(F32)
        for k in range(4):
            j = (x + k) % 4
            if k:
                arrived(j).wait_recv()
            for h in range(2):
                lanes = pl.ds(pl.multiple_of(j * 256 + h * HD, HD), HD)
                a = moe_ref[:, lanes].astype(F32)
                m = held[j, :, h * HD : (h + 1) * HD]
                g = attention_ref[:, lanes]
                given = (up_in_ref[:, lanes].astype(F32) * loss_mask).astype(BF)
                q = a * inverse_rms(a) * g
                q_high, q_low = split(q)
                scores = (dot_nt(q_high, m) + dot_nt(q_low, m)) * (1.0 / math.sqrt(HD))
                weights = jnp.exp(scores) * key_mask
                probs = weights / jnp.sum(weights, axis=-1, keepdims=True)
                rounded = probs.astype(BF)
                d_probs = dot_nt(given, m).astype(BF).astype(F32)
                inner = jnp.sum(d_probs * probs, axis=-1, keepdims=True)
                d_scores = probs * (d_probs - inner) * (1.0 / math.sqrt(HD))
                s_high, s_low = split(d_scores)
                d_q = dot(s_high, m) + dot(s_low, m)
                t_high, t_low = split(d_scores.T)
                rounded_t = rounded.astype(F32).T.astype(BF)
                d_m = (
                    dot(rounded_t, given)
                    + dot(t_high, q_high)
                    + dot(t_high, q_low)
                    + dot(t_low, q_high)
                )
                up_ref[:, lanes] = (given.astype(F32) + rms_back(a, g, d_q)).astype(BF)
                if k == 0:
                    total[:, h * HD : (h + 1) * HD] = d_m
                else:
                    terms[k, :, h * HD : (h + 1) * HD] = d_m.astype(BF)
            if k:

                @pl.when(high_z)
                def _():
                    term_high(k).start()

                @pl.when(low_z)
                def _():
                    term_low(k).start()

    def cross_copy():
        return remote(cross_out, cross_in, x_sem.at[0], x_sem.at[1], x, side)

    def final_copy():
        return remote(final_out, final_in.at[x], f_send, f_recv.at[x], 1, p)

    def final_arrived(quarter):
        return remote(final_out, final_in.at[quarter], f_send, f_recv.at[quarter], s, side)

    def far_copy():
        return remote(cross_in, far_in.at[x], r_send, r_recv.at[x], 1, side)

    def far_arrived(quarter):
        return remote(cross_in, far_in.at[quarter], r_send, r_recv.at[quarter], s, side)

    @pl.when(high_z)
    def _():
        for slot in range(3):
            term_in(slot).wait_recv()
        summed = total[...]
        for slot in range(3):
            summed = summed + terms_in[slot].astype(F32)
        cross_out[...] = summed.astype(BF)
        cross_copy().start()

    @pl.when(s < 2)
    def _():
        total[...] = jnp.zeros_like(total)

    @pl.when(low_z)
    def _():
        for slot in range(2):

            @pl.when(s != slot + 2)
            def _():
                term_in(slot).wait_recv()
                total[...] += terms_in[slot].astype(F32)

    @pl.when(sender)
    def _():
        final_out[...] = total[...].astype(BF)
        final_copy().start()

    @pl.when(low_z)
    def _():
        remote(cross_in, cross_in, x_sem.at[0], x_sem.at[1], s, side).wait_recv()
        far_copy().start()

    @pl.when(s == 0)
    def _():
        up_ref[...] = up_in_ref[...]

    @pl.when(bridge)
    def _():
        pieces = []
        for quarter in range(4):
            if quarter == 1:
                near = total[...]
            else:
                final_arrived(quarter).wait_recv()
                near = final_in[quarter].astype(F32)
            far_arrived(quarter).wait_recv()
            pieces.append(near + far_in[quarter].astype(F32))
        cotangent = jnp.concatenate(pieces, axis=1)
        v = moe_ref[...].astype(F32)
        up_ref[...] = rms_back(v, final_ref[...], cotangent).astype(BF)

    def finish():
        @pl.when(bridge)
        def _():
            for i in range(len(relays)):
                relay_copy(i).wait_send()
            for i in range(len(direct)):
                direct_copy(i).wait_send()

        @pl.when(low_z)
        def _():
            relay_on().wait_send()
            far_copy().wait_send()

        @pl.when(sender)
        def _():
            final_copy().wait_send()

        @pl.when(high_z)
        def _():
            cross_copy().wait_send()
            for d in range(1, 4):
                onward(d, 4 + (x + d) % 4).wait_send()
                term_high(d).wait_send()

        @pl.when(low_decoder)
        def _():
            for d in range(1, 4):
                term_low(d).wait_send()

    return finish


def whole_kernel(
    source_len,
    target_len,
    x_ref,
    up_in_ref,
    ids_ref,
    gates_ref,
    attention_ref,
    mixture_ref,
    final_ref,
    w_in_hbm,
    w_out_hbm,
    gate_ref,
    grad_ref,
    w_in,
    w_out,
    hidden,
    units,
    full,
    product,
    packing,
    unpacking,
    matches,
    weights,
    moe_ref,
    states_ref,
    summed_ref,
    up_ref,
    w_sem,
    *refs,
):
    cross_refs = refs[: len(CROSS_SCRATCH)]
    refs = refs[len(CROSS_SCRATCH) :]
    ahead = Exchange(refs[: len(refs) // 2])
    behind = Exchange(refs[len(refs) // 2 :])
    in_copy = pltpu.make_async_copy(w_in_hbm, w_in, w_sem.at[0])
    out_copy = pltpu.make_async_copy(w_out_hbm, w_out, w_sem.at[1])
    barrier = pltpu.get_barrier_semaphore()
    s = lax.axis_index("section")
    p = lax.axis_index("expert")
    ahead.greet()
    for d in range(1, 8):
        for other in (p, ahead.pair_partner()):
            pl.semaphore_signal(
                barrier, inc=1, device_id=((s + d) % 8, other), device_id_type=MESH
            )
    in_copy.start()
    out_copy.start()

    first, second, weighted = slot_tables(ids_ref, gates_ref)
    x = x_ref[...].astype(F32)
    normed = (x * inverse_rms(x) * mixture_ref[...]).astype(BF)
    placing_t = (first + second).T.astype(BF)
    packing[...] = pack_matrix()
    slots = pack(dot(placing_t, normed).astype(BF), packing[...])
    ahead.slots[...] = slots.reshape(EXPERTS, PAD, PACKED)
    pl.semaphore_wait(barrier, 46)
    ahead.send_out()
    matches[0] = first.astype(BF)
    matches[1] = second.astype(BF)
    weights[...] = weighted
    unpacking[...] = unpack_matrix()
    in_copy.wait()
    out_copy.wait()

    def experts(t, source):
        ahead.received(t, full, unpacking[...])
        rows = full[...]

        def up(n, carry):
            tile = pl.ds(pl.multiple_of(n * TILE, TILE), TILE)
            hidden[source, :, tile] = jnp.maximum(dot(rows, w_in[:, tile]), 0.0).astype(BF)
            return carry

        lax.fori_loop(0, D // TILE, up, 0)
        held = hidden[source]

        def down(n, carry):
            tile = pl.ds(pl.multiple_of(n * TILE, TILE), TILE)
            product[:, tile] = dot(held, w_out[:, tile]).astype(BF)
            return carry

        lax.fori_loop(0, D // TILE, down, 0)
        ahead.products[t] = pack(product[...], packing[...]).reshape(2, 2, 4, PAD, PACKED)

    ahead.run(experts)
    summed = ahead.returned(unpacking[...])
    summed_ref[...] = summed
    high, low = split(weights[...])
    moe = (x_ref[...].astype(F32) + (dot(high, summed) + dot(low, summed))).astype(BF)
    moe_ref[...] = moe

    @pl.when(s == 1)
    def _():
        wide = moe_ref[...].astype(F32)
        states = (wide * inverse_rms(wide) * final_ref[...]).astype(BF)
        for quarter in range(4):
            states_ref[quarter] = states[:, quarter * 256 : (quarter + 1) * 256]

    finish_cross = cross_part(
        source_len,
        target_len,
        states_ref,
        moe_ref,
        up_in_ref,
        attention_ref,
        final_ref,
        up_ref,
        *cross_refs,
    )

    up_low = up_ref[...]
    high, low = split(weights[...].T)
    grads = dot(high, up_low) + dot(low, up_low)
    behind.slots[...] = pack(grads.astype(BF), packing[...]).reshape(EXPERTS, PAD, PACKED)
    behind.send_out()
    wide_up = up_low.astype(F32)
    for choice in range(2):
        chosen = dot(matches[choice], summed_ref[...])
        column = jnp.sum(wide_up * chosen, axis=1, keepdims=True)
        gate_ref[choice : choice + 1, :] = jnp.broadcast_to(column, (TOK, TOK)).T[0:1, :]

    def experts_back(t, source):
        behind.received(t, full, unpacking[...])
        rows = full[...]

        def down(n, carry):
            tile = pl.ds(pl.multiple_of(n * TILE, TILE), TILE)
            part = dot_nt(rows, w_out[tile, :])
            alive = hidden[source, :, tile].astype(F32) > 0.0
            units[:, tile] = jnp.where(alive, part, 0.0).astype(BF)
            return carry

        lax.fori_loop(0, D // TILE, down, 0)
        held = units[...]

        def across(n, carry):
            tile = pl.ds(pl.multiple_of(n * TILE, TILE), TILE)
            product[:, tile] = dot_nt(held, w_in[tile, :]).astype(BF)
            return carry

        lax.fori_loop(0, D // TILE, across, 0)
        behind.products[t] = pack(product[...], packing[...]).reshape(2, 2, 4, PAD, PACKED)

    behind.run(experts_back)
    placing = (matches[0].astype(F32) + matches[1].astype(F32)).astype(BF)
    normed_grad = dot(placing, behind.returned(unpacking[...]))
    back = rms_back(x_ref[...].astype(F32), mixture_ref[...], normed_grad)
    grad_ref[...] = (up_ref[...].astype(F32) + back).astype(BF)
    ahead.finish()
    finish_cross()
    behind.finish()


VM = pl.BlockSpec(memory_space=pltpu.VMEM)
SM = pl.BlockSpec(memory_space=pltpu.SMEM)
HB = pl.BlockSpec(memory_space=pl.ANY)


def shape(dims, dtype):
    return jax.ShapeDtypeStruct(dims, dtype)


def params(number):
    return pltpu.CompilerParams(
        collective_id=number, has_side_effects=True, vmem_limit_bytes=60 * 1024 * 1024
    )


def body(
    layer_in,
    upstream,
    source_lengths,
    target_lengths,
    expert_ids,
    gate_values,
    expert_in,
    expert_out,
    attention_gain,
    mixture_gain,
    final_gain,
):
    vmem = pltpu.VMEM
    gate_grad, input_grad = pl.pallas_call(
        whole_kernel,
        out_shape=(shape((2, TOK), F32), shape((TOK, D), BF)),
        in_specs=[SM] * 2 + [VM] * 7 + [HB] * 2,
        out_specs=(VM, VM),
        scratch_shapes=[
            vmem((D, D), BF),
            vmem((D, D), BF),
            vmem((4, BLOCK, D), BF),
            vmem((BLOCK, D), BF),
            vmem((BLOCK, D), BF),
            vmem((BLOCK, D), BF),
            vmem((PACKED, 128), BF),
            vmem((128, PACKED), BF),
            vmem((2, TOK, ROWS), BF),
            vmem((TOK, ROWS), F32),
            vmem((TOK, D), BF),
            vmem((4, TOK, 256), BF),
            vmem((ROWS, D), BF),
            vmem((TOK, D), BF),
            pltpu.SemaphoreType.DMA((2,)),
        ]
        + CROSS_SCRATCH
        + Exchange.scratch
        + Exchange.scratch,
        compiler_params=params(0),
        cost_estimate=pl.CostEstimate(
            flops=8 * 1024 * 1024 * 1024, bytes_accessed=8 << 20, transcendentals=0
        ),
        name="mixture_step",
    )(
        source_lengths,
        target_lengths,
        layer_in[0],
        upstream[0],
        expert_ids[0].T,
        gate_values[0].T,
        attention_gain,
        mixture_gain,
        final_gain.reshape(1, D),
        expert_in[0],
        expert_out[0],
    )
    return (gate_grad.T[None], input_grad[None])


def solution(mesh):
    in_specs = (
        P("section", "expert", None),
        P("section", "expert", None),
        P("expert"),
        P("expert"),
        P("section", "expert", None),
        P("section", "expert", None),
        P("section", None, "expert"),
        P("section", "expert", None),
        P("section", None),
        P("section", None),
        P(),
    )
    out_specs = (P("section", "expert", None), P("section", "expert", None))
    return jax.shard_map(body, mesh=mesh, in_specs=in_specs, out_specs=out_specs, check_vma=False)
```

```python
import math

import jax
import jax.numpy as jnp
from jax import lax
from jax.experimental import pallas as pl
from jax.experimental.pallas import tpu as pltpu
from jax.sharding import PartitionSpec as P

MESH = pl.DeviceIdType.MESH
BF = jnp.bfloat16
F32 = jnp.float32
EPSILON = 1e-06
EXPERTS = 16
CAP = 13
PAD = 16
TOK = 128
D = 1024
HD = 128
PACKED = 896
ROWS = EXPERTS * PAD
BLOCK = ROWS
TILE = 256
SHIFTS = (2, 3, 1, 0)
NT = (((1,), (1,)), ((), ()))


def dot(a, b):
    return jnp.dot(a, b, preferred_element_type=F32)


def dot_nt(a, b):
    return lax.dot_general(a, b, NT, preferred_element_type=F32)


def split(v):
    high = v.astype(BF)
    return high, (v - high.astype(F32)).astype(BF)


def inverse_rms(v):
    return lax.rsqrt(jnp.mean(v * v, axis=-1, keepdims=True) + EPSILON)


def rms_back(v, g, cotangent):
    r = inverse_rms(v)
    scaled = g * cotangent
    return r * scaled - v * (r * r * r * jnp.mean(v * scaled, axis=-1, keepdims=True))


def remote(src, dst, send, recv, section, expert):
    return pltpu.make_async_remote_copy(
        src_ref=src,
        dst_ref=dst,
        send_sem=send,
        recv_sem=recv,
        device_id=(section, expert),
        device_id_type=MESH,
    )


def spread(row):
    column = jnp.broadcast_to(row, (TOK, TOK)).T
    return jnp.concatenate([column, column], axis=1)


def slot_tables(ids_ref, gates_ref):
    column = lax.broadcasted_iota(jnp.int32, (TOK, ROWS), 1)
    expert = column // PAD
    place = column - expert * PAD
    first = (spread(ids_ref[0:1, :].astype(F32)) == expert.astype(F32)).astype(F32)
    second = (spread(ids_ref[1:2, :].astype(F32)) == expert.astype(F32)).astype(F32)
    earlier = lax.broadcasted_iota(jnp.int32, (TOK, TOK), 1) < lax.broadcasted_iota(
        jnp.int32, (TOK, TOK), 0
    )
    before = dot(earlier.astype(F32).astype(BF), (first + second).astype(BF))
    kept = jnp.where(place < CAP, (before == place.astype(F32)).astype(F32), 0.0)
    first = first * kept
    second = second * kept
    weighted = first * spread(gates_ref[0:1, :]) + second * spread(gates_ref[1:2, :])
    return first, second, weighted


def pack_matrix():
    row = lax.broadcasted_iota(jnp.int32, (PACKED, 128), 0)
    column = lax.broadcasted_iota(jnp.int32, (PACKED, 128), 1)
    return pack_rule(row, column)


def unpack_matrix():
    row = lax.broadcasted_iota(jnp.int32, (128, PACKED), 0)
    column = lax.broadcasted_iota(jnp.int32, (128, PACKED), 1)
    return pack_rule(column, row)


def pack_rule(spare, plain):
    chunk = spare // 128
    inside = spare - chunk * 128
    block = inside // PAD
    place = inside - block * PAD
    slot = plain - block * PAD
    wanted = chunk + 7 * (place - CAP)
    hit = jnp.where(place == CAP, 1.0, jnp.where(place == CAP + 1, 1.0, 0.0))
    hit = jnp.where(wanted == slot, hit, 0.0)
    return jnp.where(wanted < CAP, hit, 0.0).astype(BF)


def pack(values, matrix):
    spare = (lax.broadcasted_iota(jnp.int32, (128, 128), 0) % PAD) >= CAP
    halves = []
    for half in range(2):
        part = values[half * 128 : (half + 1) * 128]
        moved = dot(matrix, part[:, PACKED:])
        chunks = [
            jnp.where(
                spare,
                moved[k * 128 : (k + 1) * 128],
                part[:, k * 128 : (k + 1) * 128].astype(F32),
            ).astype(BF)
            for k in range(7)
        ]
        halves.append(jnp.concatenate(chunks, axis=1))
    return jnp.concatenate(halves, axis=0)


def unpack_last(packed, matrix):
    halves = []
    for half in range(2):
        part = packed[half * 128 : (half + 1) * 128]
        stacked = jnp.concatenate([part[:, k * 128 : (k + 1) * 128] for k in range(7)], axis=0)
        halves.append(dot(matrix, stacked).astype(BF))
    return jnp.concatenate(halves, axis=0)


class Exchange:
    scratch = [
        pltpu.VMEM((EXPERTS, PAD, PACKED), BF),
        pltpu.VMEM((4, 2, 2, 4, PAD, PACKED), BF),
        pltpu.VMEM((4, 2, 2, 4, PAD, PACKED), BF),
        pltpu.VMEM((4, 2, 4, PAD, PACKED), BF),
        pltpu.VMEM((4, 4, PAD, PACKED), BF),
        pltpu.VMEM((4, 4, PAD, PACKED), BF),
        pltpu.VMEM((4, 4, PAD, PACKED), BF),
        pltpu.VMEM((EXPERTS, PAD, PACKED), BF),
        pltpu.SemaphoreType.DMA((4, 4)),
        pltpu.SemaphoreType.DMA((4, 4)),
        pltpu.SemaphoreType.DMA((5, 4)),
        pltpu.SemaphoreType.DMA((5, 4)),
        pltpu.SemaphoreType.DMA((4, 4)),
        pltpu.SemaphoreType.DMA((4, 4)),
    ]

    def __init__(self, refs):
        (
            self.slots,
            self.rows,
            self.products,
            self.core_part,
            self.pair_out,
            self.pair_in,
            self.sums,
            self.back,
            self.a_send,
            self.a_recv,
            self.g_send,
            self.g_recv,
            self.f_send,
            self.f_recv,
        ) = refs
        self.section = lax.axis_index("section")
        p = lax.axis_index("expert")
        self.core = p % 2
        self.half = (p // 2) % 2
        self.ez = (p // 4) % 4
        self.ey = p // 16
        self.mine = self.ey * 4 + self.ez

    def device(self, ey, ez, half, core):
        return ((ey * 4 + ez) * 2 + half) * 2 + core

    def core_partner(self):
        return self.device(self.ey, self.ez, self.half, 1 - self.core)

    def pair_partner(self):
        return self.device(self.ey, self.ez, 1 - self.half, self.core)

    def greet(self):
        barrier = pltpu.get_barrier_semaphore()
        for dz in range(4):
            for dy in range(4):
                if dz or dy:
                    other = self.device(
                        (self.ey + dy) % 4, (self.ez + dz) % 4, self.half, self.core
                    )
                    pl.semaphore_signal(
                        barrier, inc=1, device_id=(self.section, other), device_id_type=MESH
                    )
        for other in (self.core_partner(), self.pair_partner()):
            pl.semaphore_signal(
                barrier, inc=1, device_id=(self.section, other), device_id_type=MESH
            )

    def out_copy(self, t, dy):
        ey, ez = (self.ey + dy) % 4, (self.ez + SHIFTS[t]) % 4
        return remote(
            self.slots.at[ey * 4 + ez],
            self.rows.at[self.ez, self.core, self.half, self.ey],
            self.a_send.at[t, dy],
            self.a_recv.at[t, dy],
            self.section,
            self.device(ey, ez, self.half, self.core),
        )

    def source(self, t):
        return (self.ez + 4 - SHIFTS[t]) % 4

    def piece(self, t, kind):
        half = self.half if kind < 2 else 1 - self.half
        ref = self.rows.at[self.source(t), self.core, half]
        target = self.pair_partner() if kind == 0 else self.core_partner()
        return remote(
            ref, ref, self.g_send.at[kind, t], self.g_recv.at[kind, t], self.section, target
        )

    def core_copy(self, t):
        return remote(
            self.products.at[t, 1 - self.core],
            self.core_part.at[t],
            self.g_send.at[3, t],
            self.g_recv.at[3, t],
            self.section,
            self.core_partner(),
        )

    def pair_copy(self, t):
        return remote(
            self.pair_out.at[t],
            self.pair_in.at[t],
            self.g_send.at[4, t],
            self.g_recv.at[4, t],
            self.section,
            self.pair_partner(),
        )

    def back_copy(self, t, dy):
        ey = (self.ey + 4 - dy) % 4
        return remote(
            self.sums.at[t, ey],
            self.back.at[self.mine],
            self.f_send.at[t, dy],
            self.f_recv.at[t, dy],
            self.section,
            self.device(ey, self.source(t), self.half, self.core),
        )

    def far(self, t):
        return [dy for dy in range(4) if SHIFTS[t] or dy]

    def send_out(self):
        for t in range(4):
            for dy in self.far(t):
                self.out_copy(t, dy).start()
        self.rows[self.ez, self.core, self.half, self.ey] = self.slots[self.mine]

    def share(self, t):
        for dy in self.far(t):
            self.out_copy(t, dy).wait_recv()
        self.piece(t, 0).start()
        self.piece(t, 1).start()

    def pass_on(self, t):
        self.piece(t, 0).wait_recv()
        self.piece(t, 2).start()

    def multiply(self, t, experts):
        self.piece(t, 1).wait_recv()
        self.piece(t, 2).wait_recv()
        experts(t, self.source(t))
        self.core_copy(t).start()

    def core_sum(self, t):
        self.core_copy(t).wait_recv()
        other = 1 - self.half
        total = self.products[t, self.core, other].astype(F32) + self.core_part[t, other].astype(
            F32
        )
        self.pair_out[t] = total.astype(BF)
        self.pair_copy(t).start()

    def pair_sum(self, t):
        self.pair_copy(t).wait_recv()
        total = (
            self.products[t, self.core, self.half].astype(F32)
            + self.core_part[t, self.half].astype(F32)
            + self.pair_in[t].astype(F32)
        )
        self.sums[t] = total.astype(BF)
        for dy in self.far(t):
            self.back_copy(t, dy).start()
        if SHIFTS[t] == 0:
            self.back[self.mine] = self.sums[t, self.ey]

    def run(self, experts):
        for step in range(8):
            for stage, lag in (
                (self.share, 0),
                (self.pass_on, 1),
                (lambda t: self.multiply(t, experts), 2),
                (self.core_sum, 3),
                (self.pair_sum, 4),
            ):
                if 0 <= step - lag < 4:
                    stage(step - lag)
        for t in range(4):
            for dy in self.far(t):
                self.back_copy(t, dy).wait_recv()

    def finish(self):
        for t in range(4):
            for dy in self.far(t):
                self.out_copy(t, dy).wait_send()
                self.back_copy(t, dy).wait_send()
            for kind in range(3):
                self.piece(t, kind).wait_send()
            self.core_copy(t).wait_send()
            self.pair_copy(t).wait_send()

    def received(self, t, full, matrix):
        packed = self.rows[self.source(t)].reshape(BLOCK, PACKED)
        full[:, :PACKED] = packed
        full[:, PACKED:] = unpack_last(packed, matrix)

    def returned(self, matrix):
        packed = self.back[...].reshape(ROWS, PACKED)
        return jnp.concatenate([packed, unpack_last(packed, matrix)], axis=1)


CROSS_SCRATCH = [
    pltpu.VMEM((4, TOK, 256), BF),
    pltpu.VMEM((4, TOK, 256), BF),
    pltpu.VMEM((3, TOK, 256), BF),
    pltpu.VMEM((TOK, 256), BF),
    pltpu.VMEM((TOK, 256), BF),
    pltpu.VMEM((TOK, 256), BF),
    pltpu.VMEM((4, TOK, 256), BF),
    pltpu.VMEM((TOK, 256), F32),
    pltpu.SemaphoreType.DMA((10,)),
    pltpu.SemaphoreType.DMA((4,)),
    pltpu.SemaphoreType.DMA((4,)),
    pltpu.SemaphoreType.DMA((3,)),
    pltpu.SemaphoreType.DMA((2,)),
    pltpu.SemaphoreType.DMA,
    pltpu.SemaphoreType.DMA((4,)),
]


def cross_part(
    source_len,
    target_len,
    states_ref,
    moe_ref,
    up_in_ref,
    attention_ref,
    final_ref,
    up_ref,
    held,
    terms,
    terms_in,
    cross_out,
    cross_in,
    final_out,
    final_in,
    total,
    s_send,
    s_recv,
    t_send,
    t_recv,
    x_sem,
    f_send,
    f_recv,
):
    s = lax.axis_index("section")
    p = lax.axis_index("expert")
    x = s % 4
    low_z = s < 4
    high_z = s >= 4
    bridge = s == 1
    decoder = s >= 2
    low_decoder = jnp.logical_and(low_z, decoder)
    relay = jnp.logical_and(low_z, s != 1)

    first_sends = [(0, 0), (2, 2), (3, 3), (1, 5)]
    later_sends = [(0, 2), (1, 2), (3, 2), (0, 3), (1, 3), (2, 3)]
    sends = first_sends + later_sends

    def bridge_copy(i):
        quarter, target = sends[i]
        return remote(
            states_ref.at[quarter], held.at[quarter], s_send.at[i], s_recv.at[quarter], target, p
        )

    def onward(slot, target):
        return remote(held.at[x], held.at[x], s_send.at[slot], s_recv.at[x], target, p)

    def arrived(quarter):
        onto = held.at[quarter]
        return remote(onto, onto, s_send.at[0], s_recv.at[quarter], s, p)

    @pl.when(bridge)
    def _():
        for i in range(len(sends)):
            bridge_copy(i).start()

    @pl.when(relay)
    def _():
        arrived(x).wait_recv()
        onward(0, x + 4).start()

    @pl.when(high_z)
    def _():
        arrived(x).wait_recv()
        for d in range(1, 4):
            onward(d, 4 + (x + d) % 4).start()

    def term_high(k):
        return remote(
            terms.at[k], terms_in.at[k - 1], t_send.at[k], t_recv.at[k - 1], 4 + (x + k) % 4, p
        )

    def term_low(k):
        return remote(
            terms.at[k], terms_in.at[s - 2], t_send.at[k], t_recv.at[s - 2], (x + k) % 4, p
        )

    def term_in(slot):
        return remote(terms.at[0], terms_in.at[slot], t_send.at[0], t_recv.at[slot], s, p)

    @pl.when(decoder)
    def _():
        tokens = lax.broadcasted_iota(jnp.int32, (TOK, 1), 0)
        keys = lax.broadcasted_iota(jnp.int32, (1, TOK), 1)
        key_mask = (keys < source_len[0]).astype(F32)
        loss_mask = jnp.logical_or(tokens < target_len[0], s < 7).astype(F32)
        for k in range(4):
            j = (x + k) % 4
            if k:
                arrived(j).wait_recv()
            for h in range(2):
                lanes = pl.ds(pl.multiple_of(j * 256 + h * HD, HD), HD)
                a = moe_ref[:, lanes].astype(F32)
                m = held[j, :, h * HD : (h + 1) * HD]
                g = attention_ref[:, lanes]
                given = (up_in_ref[:, lanes].astype(F32) * loss_mask).astype(BF)
                q = a * inverse_rms(a) * g
                q_high, q_low = split(q)
                scores = (dot_nt(q_high, m) + dot_nt(q_low, m)) * (1.0 / math.sqrt(HD))
                weights = jnp.exp(scores) * key_mask
                probs = weights / jnp.sum(weights, axis=-1, keepdims=True)
                rounded = probs.astype(BF)
                d_probs = dot_nt(given, m).astype(BF).astype(F32)
                inner = jnp.sum(d_probs * probs, axis=-1, keepdims=True)
                d_scores = probs * (d_probs - inner) * (1.0 / math.sqrt(HD))
                s_high, s_low = split(d_scores)
                d_q = dot(s_high, m) + dot(s_low, m)
                t_high, t_low = split(d_scores.T)
                rounded_t = rounded.astype(F32).T.astype(BF)
                d_m = (
                    dot(rounded_t, given)
                    + dot(t_high, q_high)
                    + dot(t_high, q_low)
                    + dot(t_low, q_high)
                )
                up_ref[:, lanes] = (given.astype(F32) + rms_back(a, g, d_q)).astype(BF)
                if k == 0:
                    total[:, h * HD : (h + 1) * HD] = d_m
                else:
                    terms[k, :, h * HD : (h + 1) * HD] = d_m.astype(BF)
            if k:

                @pl.when(high_z)
                def _():
                    term_high(k).start()

                @pl.when(low_z)
                def _():
                    term_low(k).start()

    def cross_copy(target):
        return remote(cross_out, cross_in, x_sem.at[0], x_sem.at[1], target, p)

    def final_copy():
        return remote(final_out, final_in.at[x], f_send, f_recv.at[x], 1, p)

    def final_arrived(quarter):
        return remote(final_out, final_in.at[quarter], f_send, f_recv.at[quarter], s, p)

    @pl.when(high_z)
    def _():
        for slot in range(3):
            term_in(slot).wait_recv()
        summed = total[...]
        for slot in range(3):
            summed = summed + terms_in[slot].astype(F32)
        cross_out[...] = summed.astype(BF)
        cross_copy(x).start()
        cross_copy(x).wait_send()

    @pl.when(s < 2)
    def _():
        total[...] = jnp.zeros_like(total)

    @pl.when(low_z)
    def _():
        for slot in range(2):

            @pl.when(s != slot + 2)
            def _():
                term_in(slot).wait_recv()
                total[...] += terms_in[slot].astype(F32)

        cross_copy(s).wait_recv()
        total[...] += cross_in[...].astype(F32)

    @pl.when(relay)
    def _():
        final_out[...] = total[...].astype(BF)
        final_copy().start()
        final_copy().wait_send()

    @pl.when(s == 0)
    def _():
        up_ref[...] = up_in_ref[...]

    @pl.when(bridge)
    def _():
        pieces = []
        for quarter in range(4):
            if quarter == 1:
                pieces.append(total[...])
            else:
                final_arrived(quarter).wait_recv()
                pieces.append(final_in[quarter].astype(F32))
        cotangent = jnp.concatenate(pieces, axis=1)
        v = moe_ref[...].astype(F32)
        up_ref[...] = rms_back(v, final_ref[...], cotangent).astype(BF)
        for i in range(len(sends)):
            bridge_copy(i).wait_send()

    @pl.when(relay)
    def _():
        onward(0, x + 4).wait_send()

    @pl.when(high_z)
    def _():
        for d in range(1, 4):
            onward(d, 4 + (x + d) % 4).wait_send()
            term_high(d).wait_send()

    @pl.when(low_decoder)
    def _():
        for d in range(1, 4):
            term_low(d).wait_send()


def whole_kernel(
    source_len,
    target_len,
    x_ref,
    up_in_ref,
    ids_ref,
    gates_ref,
    attention_ref,
    mixture_ref,
    final_ref,
    w_in_hbm,
    w_out_hbm,
    gate_ref,
    grad_ref,
    w_in,
    w_out,
    hidden,
    units,
    full,
    product,
    packing,
    unpacking,
    matches,
    weights,
    moe_ref,
    states_ref,
    summed_ref,
    up_ref,
    w_sem,
    *refs,
):
    cross_refs = refs[: len(CROSS_SCRATCH)]
    refs = refs[len(CROSS_SCRATCH) :]
    ahead = Exchange(refs[: len(refs) // 2])
    behind = Exchange(refs[len(refs) // 2 :])
    in_copy = pltpu.make_async_copy(w_in_hbm, w_in, w_sem.at[0])
    out_copy = pltpu.make_async_copy(w_out_hbm, w_out, w_sem.at[1])
    barrier = pltpu.get_barrier_semaphore()
    s = lax.axis_index("section")
    p = lax.axis_index("expert")
    ahead.greet()
    for d in range(1, 8):
        pl.semaphore_signal(barrier, inc=1, device_id=((s + d) % 8, p), device_id_type=MESH)
    in_copy.start()
    out_copy.start()

    first, second, weighted = slot_tables(ids_ref, gates_ref)
    x = x_ref[...].astype(F32)
    normed = (x * inverse_rms(x) * mixture_ref[...]).astype(BF)
    placing_t = (first + second).T.astype(BF)
    packing[...] = pack_matrix()
    slots = pack(dot(placing_t, normed).astype(BF), packing[...])
    ahead.slots[...] = slots.reshape(EXPERTS, PAD, PACKED)
    pl.semaphore_wait(barrier, 24)
    ahead.send_out()
    matches[0] = first.astype(BF)
    matches[1] = second.astype(BF)
    weights[...] = weighted
    unpacking[...] = unpack_matrix()
    in_copy.wait()
    out_copy.wait()

    def experts(t, source):
        ahead.received(t, full, unpacking[...])
        rows = full[...]

        def up(n, carry):
            tile = pl.ds(pl.multiple_of(n * TILE, TILE), TILE)
            hidden[source, :, tile] = jnp.maximum(dot(rows, w_in[:, tile]), 0.0).astype(BF)
            return carry

        lax.fori_loop(0, D // TILE, up, 0)
        held = hidden[source]

        def down(n, carry):
            tile = pl.ds(pl.multiple_of(n * TILE, TILE), TILE)
            product[:, tile] = dot(held, w_out[:, tile]).astype(BF)
            return carry

        lax.fori_loop(0, D // TILE, down, 0)
        ahead.products[t] = pack(product[...], packing[...]).reshape(2, 2, 4, PAD, PACKED)

    ahead.run(experts)
    summed = ahead.returned(unpacking[...])
    summed_ref[...] = summed
    high, low = split(weights[...])
    moe = (x_ref[...].astype(F32) + (dot(high, summed) + dot(low, summed))).astype(BF)
    moe_ref[...] = moe

    @pl.when(s == 1)
    def _():
        wide = moe_ref[...].astype(F32)
        states = (wide * inverse_rms(wide) * final_ref[...]).astype(BF)
        for quarter in range(4):
            states_ref[quarter] = states[:, quarter * 256 : (quarter + 1) * 256]

    cross_part(
        source_len,
        target_len,
        states_ref,
        moe_ref,
        up_in_ref,
        attention_ref,
        final_ref,
        up_ref,
        *cross_refs,
    )

    up_low = up_ref[...]
    high, low = split(weights[...].T)
    grads = dot(high, up_low) + dot(low, up_low)
    behind.slots[...] = pack(grads.astype(BF), packing[...]).reshape(EXPERTS, PAD, PACKED)
    behind.send_out()
    wide_up = up_low.astype(F32)
    for choice in range(2):
        chosen = dot(matches[choice], summed_ref[...])
        column = jnp.sum(wide_up * chosen, axis=1, keepdims=True)
        gate_ref[choice : choice + 1, :] = jnp.broadcast_to(column, (TOK, TOK)).T[0:1, :]

    def experts_back(t, source):
        behind.received(t, full, unpacking[...])
        rows = full[...]

        def down(n, carry):
            tile = pl.ds(pl.multiple_of(n * TILE, TILE), TILE)
            part = dot_nt(rows, w_out[tile, :])
            alive = hidden[source, :, tile].astype(F32) > 0.0
            units[:, tile] = jnp.where(alive, part, 0.0).astype(BF)
            return carry

        lax.fori_loop(0, D // TILE, down, 0)
        held = units[...]

        def across(n, carry):
            tile = pl.ds(pl.multiple_of(n * TILE, TILE), TILE)
            product[:, tile] = dot_nt(held, w_in[tile, :]).astype(BF)
            return carry

        lax.fori_loop(0, D // TILE, across, 0)
        behind.products[t] = pack(product[...], packing[...]).reshape(2, 2, 4, PAD, PACKED)

    behind.run(experts_back)
    placing = (matches[0].astype(F32) + matches[1].astype(F32)).astype(BF)
    normed_grad = dot(placing, behind.returned(unpacking[...]))
    back = rms_back(x_ref[...].astype(F32), mixture_ref[...], normed_grad)
    grad_ref[...] = (up_ref[...].astype(F32) + back).astype(BF)
    ahead.finish()
    behind.finish()


VM = pl.BlockSpec(memory_space=pltpu.VMEM)
SM = pl.BlockSpec(memory_space=pltpu.SMEM)
HB = pl.BlockSpec(memory_space=pl.ANY)


def shape(dims, dtype):
    return jax.ShapeDtypeStruct(dims, dtype)


def params(number):
    return pltpu.CompilerParams(
        collective_id=number, has_side_effects=True, vmem_limit_bytes=60 * 1024 * 1024
    )


def body(
    layer_in,
    upstream,
    source_lengths,
    target_lengths,
    expert_ids,
    gate_values,
    expert_in,
    expert_out,
    attention_gain,
    mixture_gain,
    final_gain,
):
    vmem = pltpu.VMEM
    gate_grad, input_grad = pl.pallas_call(
        whole_kernel,
        out_shape=(shape((2, TOK), F32), shape((TOK, D), BF)),
        in_specs=[SM] * 2 + [VM] * 7 + [HB] * 2,
        out_specs=(VM, VM),
        scratch_shapes=[
            vmem((D, D), BF),
            vmem((D, D), BF),
            vmem((4, BLOCK, D), BF),
            vmem((BLOCK, D), BF),
            vmem((BLOCK, D), BF),
            vmem((BLOCK, D), BF),
            vmem((PACKED, 128), BF),
            vmem((128, PACKED), BF),
            vmem((2, TOK, ROWS), BF),
            vmem((TOK, ROWS), F32),
            vmem((TOK, D), BF),
            vmem((4, TOK, 256), BF),
            vmem((ROWS, D), BF),
            vmem((TOK, D), BF),
            pltpu.SemaphoreType.DMA((2,)),
        ]
        + CROSS_SCRATCH
        + Exchange.scratch
        + Exchange.scratch,
        compiler_params=params(0),
        cost_estimate=pl.CostEstimate(
            flops=8 * 1024 * 1024 * 1024, bytes_accessed=8 << 20, transcendentals=0
        ),
        name="mixture_step",
    )(
        source_lengths,
        target_lengths,
        layer_in[0],
        upstream[0],
        expert_ids[0].T,
        gate_values[0].T,
        attention_gain,
        mixture_gain,
        final_gain.reshape(1, D),
        expert_in[0],
        expert_out[0],
    )
    return (gate_grad.T[None], input_grad[None])


def solution(mesh):
    in_specs = (
        P("section", "expert", None),
        P("section", "expert", None),
        P("expert"),
        P("expert"),
        P("section", "expert", None),
        P("section", "expert", None),
        P("section", None, "expert"),
        P("section", "expert", None),
        P("section", None),
        P("section", None),
        P(),
    )
    out_specs = (P("section", "expert", None), P("section", "expert", None))
    return jax.shard_map(body, mesh=mesh, in_specs=in_specs, out_specs=out_specs, check_vma=False)
```

```python
import math

import jax
import jax.numpy as jnp
from jax import lax
from jax.experimental import pallas as pl
from jax.experimental.pallas import tpu as pltpu
from jax.sharding import PartitionSpec as P

MESH = pl.DeviceIdType.MESH
BF = jnp.bfloat16
F32 = jnp.float32
EPSILON = 1e-06
EXPERTS = 16
CAP = 13
PAD = 16
TOK = 128
D = 1024
HD = 128
PACKED = 896
ROWS = EXPERTS * PAD
BLOCK = ROWS
TILE = 512
SHIFTS = (2, 3, 1, 0)
NT = (((1,), (1,)), ((), ()))


def dot(a, b):
    return jnp.dot(a, b, preferred_element_type=F32)


def dot_nt(a, b):
    return lax.dot_general(a, b, NT, preferred_element_type=F32)


def split(v):
    high = v.astype(BF)
    return high, (v - high.astype(F32)).astype(BF)


def inverse_rms(v):
    return lax.rsqrt(jnp.mean(v * v, axis=-1, keepdims=True) + EPSILON)


def rms_back(v, g, cotangent):
    r = inverse_rms(v)
    scaled = g * cotangent
    return r * scaled - v * (r * r * r * jnp.mean(v * scaled, axis=-1, keepdims=True))


def remote(src, dst, send, recv, section, expert):
    return pltpu.make_async_remote_copy(
        src_ref=src,
        dst_ref=dst,
        send_sem=send,
        recv_sem=recv,
        device_id=(section, expert),
        device_id_type=MESH,
    )


def spread(row):
    column = jnp.broadcast_to(row, (TOK, TOK)).T
    return jnp.concatenate([column, column], axis=1)


def slot_tables(ids_ref, gates_ref):
    column = lax.broadcasted_iota(jnp.int32, (TOK, ROWS), 1)
    expert = column // PAD
    place = column - expert * PAD
    first = (spread(ids_ref[0:1, :].astype(F32)) == expert.astype(F32)).astype(F32)
    second = (spread(ids_ref[1:2, :].astype(F32)) == expert.astype(F32)).astype(F32)
    earlier = lax.broadcasted_iota(jnp.int32, (TOK, TOK), 1) < lax.broadcasted_iota(
        jnp.int32, (TOK, TOK), 0
    )
    before = dot(earlier.astype(F32).astype(BF), (first + second).astype(BF))
    kept = jnp.where(place < CAP, (before == place.astype(F32)).astype(F32), 0.0)
    first = first * kept
    second = second * kept
    weighted = first * spread(gates_ref[0:1, :]) + second * spread(gates_ref[1:2, :])
    return first, second, weighted


def pack_matrix():
    row = lax.broadcasted_iota(jnp.int32, (PACKED, 128), 0)
    column = lax.broadcasted_iota(jnp.int32, (PACKED, 128), 1)
    return pack_rule(row, column)


def unpack_matrix():
    row = lax.broadcasted_iota(jnp.int32, (128, PACKED), 0)
    column = lax.broadcasted_iota(jnp.int32, (128, PACKED), 1)
    return pack_rule(column, row)


def pack_rule(spare, plain):
    chunk = spare // 128
    inside = spare - chunk * 128
    block = inside // PAD
    place = inside - block * PAD
    slot = plain - block * PAD
    wanted = chunk + 7 * (place - CAP)
    hit = jnp.where(place == CAP, 1.0, jnp.where(place == CAP + 1, 1.0, 0.0))
    hit = jnp.where(wanted == slot, hit, 0.0)
    return jnp.where(wanted < CAP, hit, 0.0).astype(BF)


def pack(values, matrix):
    spare = (lax.broadcasted_iota(jnp.int32, (128, 128), 0) % PAD) >= CAP
    halves = []
    for half in range(2):
        part = values[half * 128 : (half + 1) * 128]
        moved = dot(matrix, part[:, PACKED:])
        chunks = [
            jnp.where(
                spare,
                moved[k * 128 : (k + 1) * 128],
                part[:, k * 128 : (k + 1) * 128].astype(F32),
            ).astype(BF)
            for k in range(7)
        ]
        halves.append(jnp.concatenate(chunks, axis=1))
    return jnp.concatenate(halves, axis=0)


def unpack_last(packed, matrix):
    halves = []
    for half in range(2):
        part = packed[half * 128 : (half + 1) * 128]
        stacked = jnp.concatenate([part[:, k * 128 : (k + 1) * 128] for k in range(7)], axis=0)
        halves.append(dot(matrix, stacked).astype(BF))
    return jnp.concatenate(halves, axis=0)


class Exchange:
    scratch = [
        pltpu.VMEM((EXPERTS, PAD, PACKED), BF),
        pltpu.VMEM((4, 2, 2, 4, PAD, PACKED), BF),
        pltpu.VMEM((4, 2, 2, 4, PAD, PACKED), BF),
        pltpu.VMEM((4, 2, 4, PAD, PACKED), BF),
        pltpu.VMEM((4, 4, PAD, PACKED), BF),
        pltpu.VMEM((4, 4, PAD, PACKED), BF),
        pltpu.VMEM((4, 4, PAD, PACKED), BF),
        pltpu.VMEM((EXPERTS, PAD, PACKED), BF),
        pltpu.SemaphoreType.DMA((4, 4)),
        pltpu.SemaphoreType.DMA((4, 4)),
        pltpu.SemaphoreType.DMA((5, 4)),
        pltpu.SemaphoreType.DMA((5, 4)),
        pltpu.SemaphoreType.DMA((4, 4)),
        pltpu.SemaphoreType.DMA((4, 4)),
    ]

    def __init__(self, refs):
        (
            self.slots,
            self.rows,
            self.products,
            self.core_part,
            self.pair_out,
            self.pair_in,
            self.sums,
            self.back,
            self.a_send,
            self.a_recv,
            self.g_send,
            self.g_recv,
            self.f_send,
            self.f_recv,
        ) = refs
        self.section = lax.axis_index("section")
        p = lax.axis_index("expert")
        self.core = p % 2
        self.half = (p // 2) % 2
        self.ez = (p // 4) % 4
        self.ey = p // 16
        self.mine = self.ey * 4 + self.ez

    def device(self, ey, ez, half, core):
        return ((ey * 4 + ez) * 2 + half) * 2 + core

    def core_partner(self):
        return self.device(self.ey, self.ez, self.half, 1 - self.core)

    def pair_partner(self):
        return self.device(self.ey, self.ez, 1 - self.half, self.core)

    def greet(self):
        barrier = pltpu.get_barrier_semaphore()
        for dz in range(4):
            for dy in range(4):
                if dz or dy:
                    other = self.device(
                        (self.ey + dy) % 4, (self.ez + dz) % 4, self.half, self.core
                    )
                    pl.semaphore_signal(
                        barrier, inc=1, device_id=(self.section, other), device_id_type=MESH
                    )
        for other in (self.core_partner(), self.pair_partner()):
            pl.semaphore_signal(
                barrier, inc=1, device_id=(self.section, other), device_id_type=MESH
            )

    def out_copy(self, t, dy):
        ey, ez = (self.ey + dy) % 4, (self.ez + SHIFTS[t]) % 4
        return remote(
            self.slots.at[ey * 4 + ez],
            self.rows.at[self.ez, self.core, self.half, self.ey],
            self.a_send.at[t, dy],
            self.a_recv.at[t, dy],
            self.section,
            self.device(ey, ez, self.half, self.core),
        )

    def source(self, t):
        return (self.ez + 4 - SHIFTS[t]) % 4

    def piece(self, t, kind):
        half = self.half if kind < 2 else 1 - self.half
        ref = self.rows.at[self.source(t), self.core, half]
        target = self.pair_partner() if kind == 0 else self.core_partner()
        return remote(
            ref, ref, self.g_send.at[kind, t], self.g_recv.at[kind, t], self.section, target
        )

    def core_copy(self, t):
        return remote(
            self.products.at[t, 1 - self.core],
            self.core_part.at[t],
            self.g_send.at[3, t],
            self.g_recv.at[3, t],
            self.section,
            self.core_partner(),
        )

    def pair_copy(self, t):
        return remote(
            self.pair_out.at[t],
            self.pair_in.at[t],
            self.g_send.at[4, t],
            self.g_recv.at[4, t],
            self.section,
            self.pair_partner(),
        )

    def back_copy(self, t, dy):
        ey = (self.ey + 4 - dy) % 4
        return remote(
            self.sums.at[t, ey],
            self.back.at[self.mine],
            self.f_send.at[t, dy],
            self.f_recv.at[t, dy],
            self.section,
            self.device(ey, self.source(t), self.half, self.core),
        )

    def far(self, t):
        return [dy for dy in range(4) if SHIFTS[t] or dy]

    def send_out(self):
        for t in range(4):
            for dy in self.far(t):
                self.out_copy(t, dy).start()
        self.rows[self.ez, self.core, self.half, self.ey] = self.slots[self.mine]

    def share(self, t):
        for dy in self.far(t):
            self.out_copy(t, dy).wait_recv()
        self.piece(t, 0).start()
        self.piece(t, 1).start()

    def pass_on(self, t):
        self.piece(t, 0).wait_recv()
        self.piece(t, 2).start()

    def multiply(self, t, experts):
        self.piece(t, 1).wait_recv()
        self.piece(t, 2).wait_recv()
        experts(t, self.source(t))
        self.core_copy(t).start()

    def core_sum(self, t):
        self.core_copy(t).wait_recv()
        other = 1 - self.half
        total = self.products[t, self.core, other].astype(F32) + self.core_part[t, other].astype(
            F32
        )
        self.pair_out[t] = total.astype(BF)
        self.pair_copy(t).start()

    def pair_sum(self, t):
        self.pair_copy(t).wait_recv()
        total = (
            self.products[t, self.core, self.half].astype(F32)
            + self.core_part[t, self.half].astype(F32)
            + self.pair_in[t].astype(F32)
        )
        self.sums[t] = total.astype(BF)
        for dy in self.far(t):
            self.back_copy(t, dy).start()
        if SHIFTS[t] == 0:
            self.back[self.mine] = self.sums[t, self.ey]

    def run(self, experts):
        def multiply(t):
            self.multiply(t, experts)

        share, pass_on, core_sum, pair_sum = self.share, self.pass_on, self.core_sum, self.pair_sum
        for stage, t in (
            (share, 0),
            (share, 3),
            (share, 1),
            (pass_on, 0),
            (share, 2),
            (pass_on, 1),
            (pass_on, 3),
            (multiply, 0),
            (pass_on, 2),
            (multiply, 1),
            (core_sum, 0),
            (multiply, 2),
            (core_sum, 1),
            (pair_sum, 0),
            (multiply, 3),
            (core_sum, 2),
            (pair_sum, 1),
            (core_sum, 3),
            (pair_sum, 2),
            (pair_sum, 3),
        ):
            stage(t)
        for t in range(4):
            for dy in self.far(t):
                self.back_copy(t, dy).wait_recv()

    def finish(self):
        for t in range(4):
            for dy in self.far(t):
                self.out_copy(t, dy).wait_send()
                self.back_copy(t, dy).wait_send()
            for kind in range(3):
                self.piece(t, kind).wait_send()
            self.core_copy(t).wait_send()
            self.pair_copy(t).wait_send()

    def received(self, t, full, matrix):
        packed = self.rows[self.source(t)].reshape(BLOCK, PACKED)
        full[:, :PACKED] = packed
        full[:, PACKED:] = unpack_last(packed, matrix)

    def returned(self, matrix):
        packed = self.back[...].reshape(ROWS, PACKED)
        return jnp.concatenate([packed, unpack_last(packed, matrix)], axis=1)


CROSS_SCRATCH = [
    pltpu.VMEM((4, TOK, 256), BF),
    pltpu.VMEM((4, TOK, 256), BF),
    pltpu.VMEM((3, TOK, 256), BF),
    pltpu.VMEM((TOK, 256), BF),
    pltpu.VMEM((TOK, 256), BF),
    pltpu.VMEM((TOK, 256), BF),
    pltpu.VMEM((4, TOK, 256), BF),
    pltpu.VMEM((TOK, 256), F32),
    pltpu.SemaphoreType.DMA((10,)),
    pltpu.SemaphoreType.DMA((4,)),
    pltpu.SemaphoreType.DMA((4,)),
    pltpu.SemaphoreType.DMA((3,)),
    pltpu.SemaphoreType.DMA((2,)),
    pltpu.SemaphoreType.DMA,
    pltpu.SemaphoreType.DMA((4,)),
]


def cross_part(
    source_len,
    target_len,
    states_ref,
    moe_ref,
    up_in_ref,
    attention_ref,
    final_ref,
    up_ref,
    held,
    terms,
    terms_in,
    cross_out,
    cross_in,
    final_out,
    final_in,
    total,
    s_send,
    s_recv,
    t_send,
    t_recv,
    x_sem,
    f_send,
    f_recv,
):
    s = lax.axis_index("section")
    p = lax.axis_index("expert")
    x = s % 4
    low_z = s < 4
    high_z = s >= 4
    bridge = s == 1
    decoder = s >= 2
    low_decoder = jnp.logical_and(low_z, decoder)
    relay = jnp.logical_and(low_z, s != 1)

    first_sends = [(0, 0), (2, 2), (3, 3), (1, 5)]
    later_sends = [(0, 2), (1, 2), (3, 2), (0, 3), (1, 3), (2, 3)]
    sends = first_sends + later_sends

    def bridge_copy(i):
        quarter, target = sends[i]
        return remote(
            states_ref.at[quarter], held.at[quarter], s_send.at[i], s_recv.at[quarter], target, p
        )

    def onward(slot, target):
        return remote(held.at[x], held.at[x], s_send.at[slot], s_recv.at[x], target, p)

    def arrived(quarter):
        onto = held.at[quarter]
        return remote(onto, onto, s_send.at[0], s_recv.at[quarter], s, p)

    @pl.when(bridge)
    def _():
        for i in range(len(sends)):
            bridge_copy(i).start()

    @pl.when(relay)
    def _():
        arrived(x).wait_recv()
        onward(0, x + 4).start()

    @pl.when(high_z)
    def _():
        arrived(x).wait_recv()
        for d in range(1, 4):
            onward(d, 4 + (x + d) % 4).start()

    def term_high(k):
        return remote(
            terms.at[k], terms_in.at[k - 1], t_send.at[k], t_recv.at[k - 1], 4 + (x + k) % 4, p
        )

    def term_low(k):
        return remote(
            terms.at[k], terms_in.at[s - 2], t_send.at[k], t_recv.at[s - 2], (x + k) % 4, p
        )

    def term_in(slot):
        return remote(terms.at[0], terms_in.at[slot], t_send.at[0], t_recv.at[slot], s, p)

    @pl.when(decoder)
    def _():
        tokens = lax.broadcasted_iota(jnp.int32, (TOK, 1), 0)
        keys = lax.broadcasted_iota(jnp.int32, (1, TOK), 1)
        key_mask = (keys < source_len[0]).astype(F32)
        loss_mask = jnp.logical_or(tokens < target_len[0], s < 7).astype(F32)
        for k in range(4):
            j = (x + k) % 4
            if k:
                arrived(j).wait_recv()
            for h in range(2):
                lanes = pl.ds(pl.multiple_of(j * 256 + h * HD, HD), HD)
                a = moe_ref[:, lanes].astype(F32)
                m = held[j, :, h * HD : (h + 1) * HD]
                g = attention_ref[:, lanes]
                given = (up_in_ref[:, lanes].astype(F32) * loss_mask).astype(BF)
                q = a * inverse_rms(a) * g
                q_high, q_low = split(q)
                scores = (dot_nt(q_high, m) + dot_nt(q_low, m)) * (1.0 / math.sqrt(HD))
                weights = jnp.exp(scores) * key_mask
                probs = weights / jnp.sum(weights, axis=-1, keepdims=True)
                rounded = probs.astype(BF)
                d_probs = dot_nt(given, m).astype(BF).astype(F32)
                inner = jnp.sum(d_probs * probs, axis=-1, keepdims=True)
                d_scores = probs * (d_probs - inner) * (1.0 / math.sqrt(HD))
                s_high, s_low = split(d_scores)
                d_q = dot(s_high, m) + dot(s_low, m)
                t_high, t_low = split(d_scores.T)
                rounded_t = rounded.astype(F32).T.astype(BF)
                d_m = (
                    dot(rounded_t, given)
                    + dot(t_high, q_high)
                    + dot(t_high, q_low)
                    + dot(t_low, q_high)
                )
                up_ref[:, lanes] = (given.astype(F32) + rms_back(a, g, d_q)).astype(BF)
                if k == 0:
                    total[:, h * HD : (h + 1) * HD] = d_m
                else:
                    terms[k, :, h * HD : (h + 1) * HD] = d_m.astype(BF)
            if k:

                @pl.when(high_z)
                def _():
                    term_high(k).start()

                @pl.when(low_z)
                def _():
                    term_low(k).start()

    def cross_copy(target):
        return remote(cross_out, cross_in, x_sem.at[0], x_sem.at[1], target, p)

    def final_copy():
        return remote(final_out, final_in.at[x], f_send, f_recv.at[x], 1, p)

    def final_arrived(quarter):
        return remote(final_out, final_in.at[quarter], f_send, f_recv.at[quarter], s, p)

    @pl.when(high_z)
    def _():
        for slot in range(3):
            term_in(slot).wait_recv()
        summed = total[...]
        for slot in range(3):
            summed = summed + terms_in[slot].astype(F32)
        cross_out[...] = summed.astype(BF)
        cross_copy(x).start()
        cross_copy(x).wait_send()

    @pl.when(s < 2)
    def _():
        total[...] = jnp.zeros_like(total)

    @pl.when(low_z)
    def _():
        for slot in range(2):

            @pl.when(s != slot + 2)
            def _():
                term_in(slot).wait_recv()
                total[...] += terms_in[slot].astype(F32)

        cross_copy(s).wait_recv()
        total[...] += cross_in[...].astype(F32)

    @pl.when(relay)
    def _():
        final_out[...] = total[...].astype(BF)
        final_copy().start()
        final_copy().wait_send()

    @pl.when(s == 0)
    def _():
        up_ref[...] = up_in_ref[...]

    @pl.when(bridge)
    def _():
        pieces = []
        for quarter in range(4):
            if quarter == 1:
                pieces.append(total[...])
            else:
                final_arrived(quarter).wait_recv()
                pieces.append(final_in[quarter].astype(F32))
        cotangent = jnp.concatenate(pieces, axis=1)
        v = moe_ref[...].astype(F32)
        up_ref[...] = rms_back(v, final_ref[...], cotangent).astype(BF)
        for i in range(len(sends)):
            bridge_copy(i).wait_send()

    @pl.when(relay)
    def _():
        onward(0, x + 4).wait_send()

    @pl.when(high_z)
    def _():
        for d in range(1, 4):
            onward(d, 4 + (x + d) % 4).wait_send()
            term_high(d).wait_send()

    @pl.when(low_decoder)
    def _():
        for d in range(1, 4):
            term_low(d).wait_send()


def whole_kernel(
    source_len,
    target_len,
    x_ref,
    up_in_ref,
    ids_ref,
    gates_ref,
    attention_ref,
    mixture_ref,
    final_ref,
    w_in_hbm,
    w_out_hbm,
    gate_ref,
    grad_ref,
    w_in,
    w_out,
    hidden,
    units,
    full,
    product,
    packing,
    unpacking,
    matches,
    weights,
    turned,
    moe_ref,
    states_ref,
    summed_ref,
    up_ref,
    w_sem,
    *refs,
):
    cross_refs = refs[: len(CROSS_SCRATCH)]
    refs = refs[len(CROSS_SCRATCH) :]
    ahead = Exchange(refs[: len(refs) // 2])
    behind = Exchange(refs[len(refs) // 2 :])
    in_copy = pltpu.make_async_copy(w_in_hbm, w_in, w_sem.at[0])
    out_copy = pltpu.make_async_copy(w_out_hbm, w_out, w_sem.at[1])
    barrier = pltpu.get_barrier_semaphore()
    s = lax.axis_index("section")
    p = lax.axis_index("expert")
    ahead.greet()
    for d in range(1, 8):
        pl.semaphore_signal(barrier, inc=1, device_id=((s + d) % 8, p), device_id_type=MESH)
    in_copy.start()
    out_copy.start()

    first, second, weighted = slot_tables(ids_ref, gates_ref)
    x = x_ref[...].astype(F32)
    normed = (x * inverse_rms(x) * mixture_ref[...]).astype(BF)
    placing_t = (first + second).T.astype(BF)
    packing[...] = pack_matrix()
    slots = pack(dot(placing_t, normed).astype(BF), packing[...])
    ahead.slots[...] = slots.reshape(EXPERTS, PAD, PACKED)
    pl.semaphore_wait(barrier, 24)
    ahead.send_out()
    matches[0] = first.astype(BF)
    matches[1] = second.astype(BF)
    weights[...] = weighted
    turned[0], turned[1] = split(weighted.T)
    unpacking[...] = unpack_matrix()
    in_copy.wait()
    out_copy.wait()

    def experts(t, source):
        ahead.received(t, full, unpacking[...])
        rows = full[...]

        def up(n, carry):
            tile = pl.ds(pl.multiple_of(n * TILE, TILE), TILE)
            hidden[source, :, tile] = jnp.maximum(dot(rows, w_in[:, tile]), 0.0).astype(BF)
            return carry

        lax.fori_loop(0, D // TILE, up, 0)
        held = hidden[source]

        def down(n, carry):
            tile = pl.ds(pl.multiple_of(n * TILE, TILE), TILE)
            product[:, tile] = dot(held, w_out[:, tile]).astype(BF)
            return carry

        lax.fori_loop(0, D // TILE, down, 0)
        ahead.products[t] = pack(product[...], packing[...]).reshape(2, 2, 4, PAD, PACKED)

    ahead.run(experts)
    summed = ahead.returned(unpacking[...])
    summed_ref[...] = summed
    high, low = split(weights[...])
    moe = (x_ref[...].astype(F32) + (dot(high, summed) + dot(low, summed))).astype(BF)
    moe_ref[...] = moe

    @pl.when(s == 1)
    def _():
        wide = moe_ref[...].astype(F32)
        states = (wide * inverse_rms(wide) * final_ref[...]).astype(BF)
        for quarter in range(4):
            states_ref[quarter] = states[:, quarter * 256 : (quarter + 1) * 256]

    cross_part(
        source_len,
        target_len,
        states_ref,
        moe_ref,
        up_in_ref,
        attention_ref,
        final_ref,
        up_ref,
        *cross_refs,
    )

    up_low = up_ref[...]
    grads = dot(turned[0], up_low) + dot(turned[1], up_low)
    behind.slots[...] = pack(grads.astype(BF), packing[...]).reshape(EXPERTS, PAD, PACKED)
    behind.send_out()
    wide_up = up_low.astype(F32)
    for choice in range(2):
        chosen = dot(matches[choice], summed_ref[...])
        column = jnp.sum(wide_up * chosen, axis=1, keepdims=True)
        gate_ref[choice : choice + 1, :] = jnp.broadcast_to(column, (TOK, TOK)).T[0:1, :]

    def experts_back(t, source):
        behind.received(t, full, unpacking[...])
        rows = full[...]

        def down(n, carry):
            tile = pl.ds(pl.multiple_of(n * TILE, TILE), TILE)
            part = dot_nt(rows, w_out[tile, :])
            alive = hidden[source, :, tile].astype(F32) > 0.0
            units[:, tile] = jnp.where(alive, part, 0.0).astype(BF)
            return carry

        lax.fori_loop(0, D // TILE, down, 0)
        held = units[...]

        def across(n, carry):
            tile = pl.ds(pl.multiple_of(n * TILE, TILE), TILE)
            product[:, tile] = dot_nt(held, w_in[tile, :]).astype(BF)
            return carry

        lax.fori_loop(0, D // TILE, across, 0)
        behind.products[t] = pack(product[...], packing[...]).reshape(2, 2, 4, PAD, PACKED)

    behind.run(experts_back)
    placing = (matches[0].astype(F32) + matches[1].astype(F32)).astype(BF)
    normed_grad = dot(placing, behind.returned(unpacking[...]))
    back = rms_back(x_ref[...].astype(F32), mixture_ref[...], normed_grad)
    grad_ref[...] = (up_ref[...].astype(F32) + back).astype(BF)
    ahead.finish()
    behind.finish()


VM = pl.BlockSpec(memory_space=pltpu.VMEM)
SM = pl.BlockSpec(memory_space=pltpu.SMEM)
HB = pl.BlockSpec(memory_space=pl.ANY)


def shape(dims, dtype):
    return jax.ShapeDtypeStruct(dims, dtype)


def params(number):
    return pltpu.CompilerParams(
        collective_id=number, has_side_effects=True, vmem_limit_bytes=60 * 1024 * 1024
    )


def body(
    layer_in,
    upstream,
    source_lengths,
    target_lengths,
    expert_ids,
    gate_values,
    expert_in,
    expert_out,
    attention_gain,
    mixture_gain,
    final_gain,
):
    vmem = pltpu.VMEM
    gate_grad, input_grad = pl.pallas_call(
        whole_kernel,
        out_shape=(shape((2, TOK), F32), shape((TOK, D), BF)),
        in_specs=[SM] * 2 + [VM] * 7 + [HB] * 2,
        out_specs=(VM, VM),
        scratch_shapes=[
            vmem((D, D), BF),
            vmem((D, D), BF),
            vmem((4, BLOCK, D), BF),
            vmem((BLOCK, D), BF),
            vmem((BLOCK, D), BF),
            vmem((BLOCK, D), BF),
            vmem((PACKED, 128), BF),
            vmem((128, PACKED), BF),
            vmem((2, TOK, ROWS), BF),
            vmem((TOK, ROWS), F32),
            vmem((2, ROWS, TOK), BF),
            vmem((TOK, D), BF),
            vmem((4, TOK, 256), BF),
            vmem((ROWS, D), BF),
            vmem((TOK, D), BF),
            pltpu.SemaphoreType.DMA((2,)),
        ]
        + CROSS_SCRATCH
        + Exchange.scratch
        + Exchange.scratch,
        compiler_params=params(0),
        cost_estimate=pl.CostEstimate(
            flops=8 * 1024 * 1024 * 1024, bytes_accessed=8 << 20, transcendentals=0
        ),
        name="mixture_step",
    )(
        source_lengths,
        target_lengths,
        layer_in[0],
        upstream[0],
        expert_ids[0].T,
        gate_values[0].T,
        attention_gain,
        mixture_gain,
        final_gain.reshape(1, D),
        expert_in[0],
        expert_out[0],
    )
    return (gate_grad.T[None], input_grad[None])


def solution(mesh):
    in_specs = (
        P("section", "expert", None),
        P("section", "expert", None),
        P("expert"),
        P("expert"),
        P("section", "expert", None),
        P("section", "expert", None),
        P("section", None, "expert"),
        P("section", "expert", None),
        P("section", None),
        P("section", None),
        P(),
    )
    out_specs = (P("section", "expert", None), P("section", "expert", None))
    return jax.shard_map(body, mesh=mesh, in_specs=in_specs, out_specs=out_specs, check_vma=False)
```
